32 devices in a mesh: blk: 8 (over z, x), col: 4 (over y, core).
Axes of the slice: x: 2, y: 2, z: 4, core: 2. Of those that a mesh axis runs over, the one named last changes fastest.
Arguments:
- density: float32 [2048, 1024], P('blk'), may hold values from -0.1875 to 0.1875
- occupied_p: int32 [16, 8], P('blk'), may hold values 0 or 1
- hamil_dens: float32 [1024, 2048], P('blk', 'col'), may hold values from -6 to 6
- occupied_hp: int32 [8, 16], P('blk', 'col'), may hold values 0 or 1
- window_sizes: int32 [8], replicated, may hold values from 64 to 128
- row_window_sizes: int32 [16], replicated, may hold values from 64 to 128
- slab_index: int32 [16], P('col'), may hold values from 0 to 781
- group_sizes: int32 [782], replicated, may hold values from 64 to 128
Outputs:
- product: float32 [2048, 2048], P('blk', 'col')
- norm_sq: float32 [], replicated
The draws below stay inside these ranges and needn't reach their ends.
All inputs are finite; a program needn't handle non-finite values. No bound on the sum of `occupied_p` or of `occupied_hp` on one device may be relied on, other than what follows from the above.
Results may differ from the reference program's by a relative error of at most 0.000068.
Values sent between devices are 32-bit elements; how exact they have to be, the bound alone decides.
A program may use at most 64 MiB of HBM per device.

```python
import jax
import jax.numpy as jnp
from jax import lax

BS = 128
NGROUP = 782
NB = 8
NR = 16
SC = 16


def with_ends(result, own_key, low, high):
    extent = result.shape
    index_at = [jax.random.randint(jax.random.fold_in(own_key, axis), (), 0, extent[axis]) for axis in range(len(extent))]
    result = result.at[tuple(index_at)].set(low)
    longest = extent.index(max(extent))
    index_at[longest] = (index_at[longest] + 1) % extent[longest]
    return result.at[tuple(index_at)].set(high)


def level_of(own_key, dims, cuts, low, high):
    gain, own = 1.0, jax.random.fold_in(own_key, 6)
    for position, blocks in cuts:
        heights = jnp.exp(jax.random.uniform(jax.random.fold_in(own, position), (blocks,), jnp.float32, low / len(cuts), high / len(cuts)))
        gain = gain * jnp.repeat(heights, dims[position] // blocks).reshape([-1 if axis == position else 1 for axis in range(len(dims))])
    return gain


def bell_draw(own_key, extent, spread, limit, pieces=(), kind=jnp.bfloat16):
    factor_of = level_of(own_key, extent, pieces, -0.22, 0.18) if pieces else 1.0
    result = jax.random.normal(own_key, extent, jnp.float32) * spread * factor_of
    return jnp.minimum(jnp.maximum(result, -limit), limit).astype(kind)


def setup_inputs(seed: int = 0) -> dict:
    key_list = jax.random.split(jax.random.key(seed), 9)
    return {
        "density": bell_draw(key_list[0], (NR * BS, NB * BS), (NB * BS) ** -0.5, 0.1875, ((0, 8),), jnp.float32),
        "occupied_p": with_ends((jax.random.randint(key_list[1], (NR, NB), 0, 2) < 1).astype(jnp.int32), jax.random.fold_in(key_list[1], 1), 0, 1),
        "hamil_dens": bell_draw(key_list[2], (NB * BS, SC * BS), 1.0, 6.0, ((0, 8), (1, 4)), jnp.float32),
        "occupied_hp": with_ends((jax.random.randint(key_list[3], (NB, SC), 0, 2) < 1).astype(jnp.int32), jax.random.fold_in(key_list[3], 1), 0, 1),
        "window_sizes": with_ends(jax.random.randint(key_list[4], (NB,), BS // 2, BS + 1), jax.random.fold_in(key_list[4], 1), BS // 2, BS).astype(jnp.int32),
        "row_window_sizes": with_ends(jax.random.randint(key_list[5], (NR,), BS // 2, BS + 1), jax.random.fold_in(key_list[5], 1), BS // 2, BS).astype(jnp.int32),
        "slab_index": with_ends(jax.random.randint(key_list[6], (SC,), 0, NGROUP), jax.random.fold_in(key_list[6], 1), 0, NGROUP - 1).astype(jnp.int32),
        "group_sizes": with_ends(jax.random.randint(key_list[7], (NGROUP,), BS // 2, BS + 1), jax.random.fold_in(key_list[7], 1), BS // 2, BS).astype(jnp.int32),
    }


def reference(density, occupied_p, hamil_dens, occupied_hp, window_sizes, row_window_sizes, slab_index, group_sizes):
    offsets = jnp.arange(BS, dtype=jnp.int32)
    row_live = (offsets[None, :] < row_window_sizes[:, None]).astype(jnp.float32).reshape(-1)
    inner_live = (offsets[None, :] < window_sizes[:, None]).astype(jnp.float32).reshape(-1)
    slab_sizes = group_sizes[slab_index]
    col_live = (offsets[None, :] < slab_sizes[:, None]).astype(jnp.float32).reshape(-1)
    occ_p = jnp.repeat(jnp.repeat(occupied_p.astype(jnp.float32), BS, axis=0), BS, axis=1)
    occ_hp = jnp.repeat(jnp.repeat(occupied_hp.astype(jnp.float32), BS, axis=0), BS, axis=1)
    p_eff = density * occ_p * row_live[:, None] * inner_live[None, :]
    hp_eff = hamil_dens * occ_hp * inner_live[:, None] * col_live[None, :]
    product = jnp.dot(p_eff, hp_eff, precision=lax.Precision.HIGHEST, preferred_element_type=jnp.float32)
    norm_sq = jnp.sum(product * product)
    return product, norm_sq
```

```python
import functools

import jax
import jax.numpy as jnp
from jax import lax
from jax.experimental import pallas as pl
from jax.experimental.pallas import tpu as pltpu
from jax.sharding import PartitionSpec as P

MESH = pl.DeviceIdType.MESH
PAIR = 2
CHUNKS = 4
EXTRA = 2


def kernel(
    length,
    cols,
    density,
    hamil_in,
    occ_p_in,
    occ_hp_in,
    window_in,
    row_window_in,
    slab_in,
    groups_in,
    product,
    norm,
    hamil,
    occ_p,
    occ_hp,
    window,
    row_window,
    slab,
    groups,
    gathered,
    p_in,
    p_high,
    p_low,
    parts,
    send_sem,
    recv_sem,
    load_sem,
    part_send,
    part_recv,
):
    count = length * PAIR
    total = count * cols
    block, width = hamil.shape
    row_blocks = product.shape[0] // block
    panels = width // block
    piece = block // CHUNKS
    me = lax.axis_index("blk")
    my_col = lax.axis_index("col")
    z = me // PAIR
    x = me % PAIR
    partner = me + 1 - 2 * x
    last = length - 1
    has_up = z < last
    has_down = z > 0

    loads = [
        pltpu.make_async_copy(source, target, load_sem.at[at])
        for at, (source, target) in enumerate(
            (
                (occ_hp_in, occ_hp),
                (window_in, window),
                (slab_in, slab),
                (groups_in, groups),
                (row_window_in, row_window),
                (occ_p_in, occ_p),
                (density, p_in),
            )
        )
    ]
    hamil_loads = [
        pltpu.make_async_copy(
            hamil_in.at[pl.ds(chunk * piece, piece)],
            hamil.at[pl.ds(chunk * piece, piece)],
            load_sem.at[len(loads) + chunk],
        )
        for chunk in range(CHUNKS)
    ]
    barrier = pltpu.get_barrier_semaphore()

    def greet(device):
        pl.semaphore_signal(barrier, inc=1, device_id=device, device_id_type=MESH)

    greet({"blk": partner})

    @pl.when(has_up)
    def _():
        greet({"blk": me + PAIR})

    @pl.when(has_down)
    def _():
        greet({"blk": me - PAIR})

    @pl.loop(1, cols)
    def greet_col(step):
        greet({"col": (my_col + step) % cols})

    for load in loads[:4] + hamil_loads + loads[4:]:
        load.start()

    for load in loads[:4]:
        load.wait()

    def move(where, k, chunk, device):
        rows = gathered.at[k, pl.ds(chunk * piece, piece), :]
        return pltpu.make_async_remote_copy(
            src_ref=rows,
            dst_ref=rows,
            send_sem=send_sem.at[where, k, chunk],
            recv_sem=recv_sem.at[k, chunk],
            device_id={"blk": device},
            device_id_type=MESH,
        )

    def up(k, chunk):
        return move(0, k, chunk, me + PAIR)

    def down(k, chunk):
        return move(1, k, chunk, me - PAIR)

    def across(k, chunk):
        return move(2, k, chunk, partner)

    piece_row = lax.broadcasted_iota(jnp.int32, (piece, block), 0)
    piece_col = lax.broadcasted_iota(jnp.int32, (piece, block), 1)
    order = list(range(EXTRA, CHUNKS)) + list(range(EXTRA))
    for at, chunk in enumerate(order):
        hamil_loads[chunk].wait()
        there = pl.ds(chunk * piece, piece)
        rows_live = piece_row + chunk * piece < window[me]
        for panel in range(panels):
            size = groups[slab[panel]]
            occupied = occ_hp[0, panel].astype(jnp.float32)
            mask = jnp.where(rows_live & (piece_col < size), occupied, 0.0)
            here = pl.ds(panel * block, block)
            gathered[me, there, here] = hamil[there, here] * mask
        if at == 0:
            ends = jnp.int32(z == 0) + jnp.int32(z == last)
            pl.semaphore_wait(barrier, PAIR - 1 + cols - 1 + 2 - ends)

        across(me, chunk).start()

        @pl.when(has_up)
        def _():
            up(me, chunk).start()

        @pl.when(has_down)
        def _():
            down(me, chunk).start()

    for load in loads[4:]:
        load.wait()

    row_at = lax.broadcasted_iota(jnp.int32, (block, block), 0)
    col_at = lax.broadcasted_iota(jnp.int32, (block, block), 1)

    @pl.loop(0, length)
    def split(at):
        for b in range(row_blocks):
            live = row_at < row_window[me * row_blocks + b]
            here = pl.ds(b * block, block)
            for other in range(PAIR):
                k = at * PAIR + other
                mask = jnp.where(
                    live & (col_at < window[k]), occ_p[b, k].astype(jnp.float32), 0.0
                )
                value = p_in[here, pl.ds(pl.multiple_of(k * block, block), block)] * mask
                high = value.astype(jnp.bfloat16)
                there = pl.ds(other * block, block)
                p_high[at, here, there] = high
                p_low[at, here, there] = (value - high.astype(jnp.float32)).astype(jnp.bfloat16)

    def times(a, b):
        return jnp.dot(a, b, preferred_element_type=jnp.float32)

    def term(at, first):
        for chunk in range(CHUNKS):
            if chunk < EXTRA:

                @pl.when((at > 0) & (at < last))
                def _():
                    across(at * PAIR + 1 - x, chunk).wait_recv()

            else:
                across(at * PAIR + 1 - x, chunk).wait_recv()
        right = gathered[pl.ds(at * PAIR, PAIR)].reshape(PAIR * block, width)
        high = right.astype(jnp.bfloat16)
        low = (right - high.astype(jnp.float32)).astype(jnp.bfloat16)
        left = p_high[at]
        value = times(left, low) + times(p_low[at], high) + times(left, high)
        product[...] = value if first else product[...] + value

    def pass_line(distance):
        for chunk in order:

            @pl.when(z - distance >= 0)
            def _():
                k = me - distance * PAIR
                across(k, chunk).wait_recv()

                @pl.when(has_up)
                def _():
                    up(k, chunk).start()

                if chunk < EXTRA:

                    @pl.when(z != distance)
                    def _():
                        across(k, chunk).start()

                else:
                    across(k, chunk).start()

            @pl.when(z + distance < length)
            def _():
                k = me + distance * PAIR
                across(k, chunk).wait_recv()

                @pl.when(has_down)
                def _():
                    down(k, chunk).start()

                if chunk < EXTRA:

                    @pl.when(z + distance != last)
                    def _():
                        across(k, chunk).start()

                else:
                    across(k, chunk).start()

    def pass_ends(distance):
        for chunk in range(EXTRA):

            @pl.when(z == distance)
            def _():
                k = 1 - x
                across(k, chunk).wait_recv()

                @pl.when(has_up)
                def _():
                    up(k, chunk).start()

            if length > 1:

                @pl.when(z + distance == last)
                def _():
                    k = last * PAIR + 1 - x
                    across(k, chunk).wait_recv()

                    @pl.when(has_down)
                    def _():
                        down(k, chunk).start()

    def add_terms(distance):
        @pl.when(z - distance >= 0)
        def _():
            term(z - distance, False)

        @pl.when(z + distance < length)
        def _():
            term(z + distance, False)

    if length > 1:
        pass_line(1)
    pass_ends(0)
    term(z, True)

    @pl.loop(2, length)
    def steps(distance):
        pass_line(distance)
        pass_ends(distance - 1)
        add_terms(distance - 1)

    if length > 1:
        pass_ends(last)
        add_terms(last)

    lane = 128
    squares = product[...] * product[...]
    squares = jnp.sum(squares.reshape(squares.shape[0] // 8, 8, width), axis=0)
    mine = squares[:, :lane]
    for panel in range(1, width // lane):
        mine = mine + squares[:, panel * lane : (panel + 1) * lane]
    spot = me * cols + my_col
    parts[spot] = mine

    def part(slot, device):
        return pltpu.make_async_remote_copy(
            src_ref=parts.at[slot],
            dst_ref=parts.at[slot],
            send_sem=part_send.at[device],
            recv_sem=part_recv.at[slot],
            device_id={"blk": device // cols, "col": device % cols},
            device_id_type=MESH,
        )

    @pl.loop(1, total)
    def send_parts(step):
        part(spot, (spot + step) % total).start()

    @pl.loop(0, length)
    def sent(at):
        k = at * PAIR + x
        end = ((at == 0) | (at == last)) & (at != z)
        for chunk in range(CHUNKS):

            @pl.when(has_up & (at <= z))
            def _():
                up(k, chunk).wait_send()

            @pl.when(has_down & (at >= z))
            def _():
                down(k, chunk).wait_send()

            if chunk < EXTRA:

                @pl.when(jnp.logical_not(end))
                def _():
                    across(k, chunk).wait_send()

            else:
                across(k, chunk).wait_send()

    for chunk in range(EXTRA):

        @pl.when(has_up)
        def _():
            up(1 - x, chunk).wait_send()

        @pl.when(has_down)
        def _():
            down(last * PAIR + 1 - x, chunk).wait_send()

    @pl.loop(1, total)
    def get_parts(step):
        other = (spot + step) % total
        part(other, other).wait_recv()

    norm[0] = jnp.sum(jnp.sum(parts[...], axis=0))

    @pl.loop(1, total)
    def sent_parts(step):
        part(spot, (spot + step) % total).wait_send()


def solution(mesh):
    count = mesh.shape["blk"]
    cols = mesh.shape["col"]
    length = count // PAIR

    def per_device(
        density,
        occupied_p,
        hamil_dens,
        occupied_hp,
        window_sizes,
        row_window_sizes,
        slab_index,
        group_sizes,
    ):
        rows, inner = density.shape
        block, width = hamil_dens.shape
        hbm = pl.BlockSpec(memory_space=pltpu.HBM)
        vmem = pl.BlockSpec(memory_space=pltpu.VMEM)
        smem = pl.BlockSpec(memory_space=pltpu.SMEM)
        product, norm = pl.pallas_call(
            functools.partial(kernel, length, cols),
            out_shape=(
                pltpu.VMEM((rows, width), jnp.float32),
                jax.ShapeDtypeStruct((1,), jnp.float32),
            ),
            in_specs=[hbm] * 8,
            out_specs=(vmem, smem),
            scratch_shapes=[
                pltpu.VMEM((block, width), jnp.float32),
                pltpu.SMEM(occupied_p.shape, jnp.int32),
                pltpu.SMEM(occupied_hp.shape, jnp.int32),
                pltpu.SMEM(window_sizes.shape, jnp.int32),
                pltpu.SMEM(row_window_sizes.shape, jnp.int32),
                pltpu.SMEM(slab_index.shape, jnp.int32),
                pltpu.SMEM(group_sizes.shape, jnp.int32),
                pltpu.VMEM((count, block, width), jnp.float32),
                pltpu.VMEM((rows, inner), jnp.float32),
                pltpu.VMEM((length, rows, PAIR * block), jnp.bfloat16),
                pltpu.VMEM((length, rows, PAIR * block), jnp.bfloat16),
                pltpu.VMEM((count * cols, 8, 128), jnp.float32),
                pltpu.SemaphoreType.DMA((3, count, CHUNKS)),
                pltpu.SemaphoreType.DMA((count, CHUNKS)),
                pltpu.SemaphoreType.DMA((7 + CHUNKS,)),
                pltpu.SemaphoreType.DMA((count * cols,)),
                pltpu.SemaphoreType.DMA((count * cols,)),
            ],
            compiler_params=pltpu.CompilerParams(
                collective_id=0, has_side_effects=True, vmem_limit_bytes=56 << 20
            ),
        )(
            *(
                pltpu.with_memory_space_constraint(value, pltpu.HBM)
                for value in (
                    density,
                    hamil_dens,
                    occupied_p,
                    occupied_hp,
                    window_sizes,
                    row_window_sizes,
                    slab_index,
                    group_sizes,
                )
            )
        )
        return product, norm.reshape(())

    return jax.shard_map(
        per_device,
        mesh=mesh,
        in_specs=(
            P("blk", None),
            P("blk", None),
            P("blk", "col"),
            P("blk", "col"),
            P(),
            P(),
            P("col"),
            P(),
        ),
        out_specs=(P("blk", "col"), P()),
        check_vma=False,
    )
```

```python
import functools

import jax
import jax.numpy as jnp
from jax import lax
from jax.experimental import pallas as pl
from jax.experimental.pallas import tpu as pltpu
from jax.sharding import PartitionSpec as P

MESH = pl.DeviceIdType.MESH
PAIR = 2
CHUNKS = 4
EXTRA = 2


def kernel(
    length,
    cols,
    density,
    hamil_in,
    occ_p_in,
    occ_hp_in,
    window_in,
    row_window_in,
    slab_in,
    groups_in,
    product,
    norm,
    hamil,
    occ_p,
    occ_hp,
    window,
    row_window,
    slab,
    groups,
    gathered,
    p_in,
    p_high,
    p_low,
    parts,
    send_sem,
    recv_sem,
    load_sem,
    part_send,
    part_recv,
):
    count = length * PAIR
    total = count * cols
    block, width = hamil.shape
    row_blocks = product.shape[0] // block
    panels = width // block
    piece = block // CHUNKS
    me = lax.axis_index("blk")
    my_col = lax.axis_index("col")
    z = me // PAIR
    x = me % PAIR
    partner = me + 1 - 2 * x
    last = length - 1
    has_up = z < last
    has_down = z > 0

    loads = [
        pltpu.make_async_copy(source, target, load_sem.at[at])
        for at, (source, target) in enumerate(
            (
                (occ_hp_in, occ_hp),
                (window_in, window),
                (slab_in, slab),
                (groups_in, groups),
                (row_window_in, row_window),
                (occ_p_in, occ_p),
                (density, p_in),
            )
        )
    ]
    hamil_loads = [
        pltpu.make_async_copy(
            hamil_in.at[pl.ds(chunk * piece, piece)],
            hamil.at[pl.ds(chunk * piece, piece)],
            load_sem.at[len(loads) + chunk],
        )
        for chunk in range(CHUNKS)
    ]
    barrier = pltpu.get_barrier_semaphore()

    def greet(device):
        pl.semaphore_signal(barrier, inc=1, device_id=device, device_id_type=MESH)

    greet({"blk": partner})

    @pl.when(has_up)
    def _():
        greet({"blk": me + PAIR})

    @pl.when(has_down)
    def _():
        greet({"blk": me - PAIR})

    @pl.loop(1, cols)
    def greet_col(step):
        greet({"col": (my_col + step) % cols})

    for load in loads[:4] + hamil_loads + loads[4:]:
        load.start()

    for load in loads[:4]:
        load.wait()

    def move(where, k, chunk, device):
        rows = gathered.at[k, pl.ds(chunk * piece, piece), :]
        return pltpu.make_async_remote_copy(
            src_ref=rows,
            dst_ref=rows,
            send_sem=send_sem.at[where, k],
            recv_sem=recv_sem.at[k, chunk],
            device_id={"blk": device},
            device_id_type=MESH,
        )

    def wait_sent(where, k, first, chunks):
        rows = gathered.at[k, pl.ds(first * piece, chunks * piece), :]
        pltpu.make_async_copy(rows, rows, send_sem.at[where, k]).wait()

    def up(k, chunk):
        return move(0, k, chunk, me + PAIR)

    def down(k, chunk):
        return move(1, k, chunk, me - PAIR)

    def across(k, chunk):
        return move(2, k, chunk, partner)

    piece_row = lax.broadcasted_iota(jnp.int32, (piece, block), 0)
    piece_col = lax.broadcasted_iota(jnp.int32, (piece, block), 1)
    order = list(range(EXTRA, CHUNKS)) + list(range(EXTRA))
    for at, chunk in enumerate(order):
        hamil_loads[chunk].wait()
        there = pl.ds(chunk * piece, piece)
        rows_live = piece_row + chunk * piece < window[me]
        for panel in range(panels):
            size = groups[slab[panel]]
            occupied = occ_hp[0, panel].astype(jnp.float32)
            mask = jnp.where(rows_live & (piece_col < size), occupied, 0.0)
            here = pl.ds(panel * block, block)
            gathered[me, there, here] = hamil[there, here] * mask
        if at == 0:
            ends = jnp.int32(z == 0) + jnp.int32(z == last)
            pl.semaphore_wait(barrier, PAIR - 1 + cols - 1 + 2 - ends)

        across(me, chunk).start()

        @pl.when(has_up)
        def _():
            up(me, chunk).start()

        @pl.when(has_down)
        def _():
            down(me, chunk).start()

    for load in loads[4:]:
        load.wait()

    row_at = lax.broadcasted_iota(jnp.int32, (block, block), 0)
    col_at = lax.broadcasted_iota(jnp.int32, (block, block), 1)

    @pl.loop(0, length)
    def split(at):
        for b in range(row_blocks):
            live = row_at < row_window[me * row_blocks + b]
            here = pl.ds(b * block, block)
            for other in range(PAIR):
                k = at * PAIR + other
                mask = jnp.where(
                    live & (col_at < window[k]), occ_p[b, k].astype(jnp.float32), 0.0
                )
                value = p_in[here, pl.ds(pl.multiple_of(k * block, block), block)] * mask
                high = value.astype(jnp.bfloat16)
                there = pl.ds(other * block, block)
                p_high[at, here, there] = high
                p_low[at, here, there] = (value - high.astype(jnp.float32)).astype(jnp.bfloat16)

    def times(a, b):
        return jnp.dot(a, b, preferred_element_type=jnp.float32)

    def term(at, first):
        for chunk in range(CHUNKS):
            if chunk < EXTRA:

                @pl.when((at > 0) & (at < last))
                def _():
                    across(at * PAIR + 1 - x, chunk).wait_recv()

            else:
                across(at * PAIR + 1 - x, chunk).wait_recv()
        right = gathered[pl.ds(at * PAIR, PAIR)].reshape(PAIR * block, width)
        high = right.astype(jnp.bfloat16)
        low = (right - high.astype(jnp.float32)).astype(jnp.bfloat16)
        left = p_high[at]
        value = times(left, low) + times(p_low[at], high) + times(left, high)
        product[...] = value if first else product[...] + value

    def pass_line(distance):
        for chunk in order:

            @pl.when(z - distance >= 0)
            def _():
                k = me - distance * PAIR
                across(k, chunk).wait_recv()

                @pl.when(has_up)
                def _():
                    up(k, chunk).start()

                if chunk < EXTRA:

                    @pl.when(z != distance)
                    def _():
                        across(k, chunk).start()

                else:
                    across(k, chunk).start()

            @pl.when(z + distance < length)
            def _():
                k = me + distance * PAIR
                across(k, chunk).wait_recv()

                @pl.when(has_down)
                def _():
                    down(k, chunk).start()

                if chunk < EXTRA:

                    @pl.when(z + distance != last)
                    def _():
                        across(k, chunk).start()

                else:
                    across(k, chunk).start()

    def pass_ends(distance):
        for chunk in range(EXTRA):

            @pl.when(z == distance)
            def _():
                k = 1 - x
                across(k, chunk).wait_recv()

                @pl.when(has_up)
                def _():
                    up(k, chunk).start()

            if length > 1:

                @pl.when(z + distance == last)
                def _():
                    k = last * PAIR + 1 - x
                    across(k, chunk).wait_recv()

                    @pl.when(has_down)
                    def _():
                        down(k, chunk).start()

    def add_terms(distance):
        @pl.when(z - distance >= 0)
        def _():
            term(z - distance, False)

        @pl.when(z + distance < length)
        def _():
            term(z + distance, False)

    if length > 1:
        pass_line(1)
    pass_ends(0)
    term(z, True)

    def half_term(at, side):
        k = at * PAIR + side
        if side is not x:
            for chunk in range(EXTRA, CHUNKS):
                across(k, chunk).wait_recv()
        right = gathered[k]
        high = right.astype(jnp.bfloat16)
        low = (right - high.astype(jnp.float32)).astype(jnp.bfloat16)
        here = pl.ds(pl.multiple_of(side * block, block), block)
        left = p_high[at, :, here]
        value = times(left, low) + times(p_low[at, :, here], high) + times(left, high)
        product[...] = product[...] + value

    @pl.loop(2, length)
    def steps(distance):
        pass_line(distance)
        pass_ends(distance - 1)
        add_terms(distance - 1)

    if length > 1:
        for end in (0, last):

            @pl.when(z == last - end)
            def _():
                half_term(end, x)

        pass_ends(last)

    @pl.loop(0, length)
    def sent(at):
        k = at * PAIR + x
        end = ((at == 0) | (at == last)) & (at != z)

        @pl.when(has_up & (at <= z))
        def _():
            wait_sent(0, k, 0, CHUNKS)

        @pl.when(has_down & (at >= z))
        def _():
            wait_sent(1, k, 0, CHUNKS)

        @pl.when(end)
        def _():
            wait_sent(2, k, EXTRA, CHUNKS - EXTRA)

        @pl.when(jnp.logical_not(end))
        def _():
            wait_sent(2, k, 0, CHUNKS)

    @pl.when(has_up)
    def _():
        wait_sent(0, 1 - x, 0, EXTRA)

    @pl.when(has_down)
    def _():
        wait_sent(1, last * PAIR + 1 - x, 0, EXTRA)

    if length > 1:
        for end in (0, last):

            @pl.when(z == last - end)
            def _():
                half_term(end, 1 - x)

    lane = 128
    squares = product[...] * product[...]
    squares = jnp.sum(squares.reshape(squares.shape[0] // 8, 8, width), axis=0)
    mine = squares[:, :lane]
    for panel in range(1, width // lane):
        mine = mine + squares[:, panel * lane : (panel + 1) * lane]
    spot = me * cols + my_col
    parts[spot, 0:1] = jnp.sum(mine, axis=0, keepdims=True)

    def part(slot, device):
        return pltpu.make_async_remote_copy(
            src_ref=parts.at[slot, pl.ds(0, 1)],
            dst_ref=parts.at[slot, pl.ds(0, 1)],
            send_sem=part_send.at[device],
            recv_sem=part_recv.at[slot],
            device_id={"blk": device // cols, "col": device % cols},
            device_id_type=MESH,
        )

    @pl.loop(1, total)
    def send_parts(step):
        part(spot, (spot + step) % total).start()

    @pl.loop(1, total)
    def get_parts(step):
        other = (spot + step) % total
        part(other, other).wait_recv()

    norm[0] = jnp.sum(parts[:, 0, :])

    @pl.loop(1, total)
    def sent_parts(step):
        part(spot, (spot + step) % total).wait_send()


def solution(mesh):
    count = mesh.shape["blk"]
    cols = mesh.shape["col"]
    length = count // PAIR

    def per_device(
        density,
        occupied_p,
        hamil_dens,
        occupied_hp,
        window_sizes,
        row_window_sizes,
        slab_index,
        group_sizes,
    ):
        rows, inner = density.shape
        block, width = hamil_dens.shape
        hbm = pl.BlockSpec(memory_space=pltpu.HBM)
        vmem = pl.BlockSpec(memory_space=pltpu.VMEM)
        smem = pl.BlockSpec(memory_space=pltpu.SMEM)
        product, norm = pl.pallas_call(
            functools.partial(kernel, length, cols),
            out_shape=(
                pltpu.VMEM((rows, width), jnp.float32),
                jax.ShapeDtypeStruct((1,), jnp.float32),
            ),
            in_specs=[hbm] * 8,
            out_specs=(vmem, smem),
            scratch_shapes=[
                pltpu.VMEM((block, width), jnp.float32),
                pltpu.SMEM(occupied_p.shape, jnp.int32),
                pltpu.SMEM(occupied_hp.shape, jnp.int32),
                pltpu.SMEM(window_sizes.shape, jnp.int32),
                pltpu.SMEM(row_window_sizes.shape, jnp.int32),
                pltpu.SMEM(slab_index.shape, jnp.int32),
                pltpu.SMEM(group_sizes.shape, jnp.int32),
                pltpu.VMEM((count, block, width), jnp.float32),
                pltpu.VMEM((rows, inner), jnp.float32),
                pltpu.VMEM((length, rows, PAIR * block), jnp.bfloat16),
                pltpu.VMEM((length, rows, PAIR * block), jnp.bfloat16),
                pltpu.VMEM((count * cols, 8, 128), jnp.float32),
                pltpu.SemaphoreType.DMA((3, count)),
                pltpu.SemaphoreType.DMA((count, CHUNKS)),
                pltpu.SemaphoreType.DMA((7 + CHUNKS,)),
                pltpu.SemaphoreType.DMA((count * cols,)),
                pltpu.SemaphoreType.DMA((count * cols,)),
            ],
            compiler_params=pltpu.CompilerParams(
                collective_id=0, has_side_effects=True, vmem_limit_bytes=56 << 20
            ),
        )(
            *(
                pltpu.with_memory_space_constraint(value, pltpu.HBM)
                for value in (
                    density,
                    hamil_dens,
                    occupied_p,
                    occupied_hp,
                    window_sizes,
                    row_window_sizes,
                    slab_index,
                    group_sizes,
                )
            )
        )
        return product, norm.reshape(())

    return jax.shard_map(
        per_device,
        mesh=mesh,
        in_specs=(
            P("blk", None),
            P("blk", None),
            P("blk", "col"),
            P("blk", "col"),
            P(),
            P(),
            P("col"),
            P(),
        ),
        out_specs=(P("blk", "col"), P()),
        check_vma=False,
    )
```

```python
import functools

import jax
import jax.numpy as jnp
from jax import lax
from jax.experimental import pallas as pl
from jax.experimental.pallas import tpu as pltpu
from jax.sharding import PartitionSpec as P

MESH = pl.DeviceIdType.MESH
PAIR = 2
CHUNKS = 4
EXTRA = 2
HALF = 512


def kernel(
    length,
    cols,
    density,
    hamil_in,
    occ_p_in,
    occ_hp_in,
    window_in,
    row_window_in,
    slab_in,
    groups_in,
    product,
    norm,
    hamil,
    occ_p,
    occ_hp,
    window,
    row_window,
    slab,
    groups,
    gathered,
    p_in,
    p_high,
    p_low,
    parts,
    send_sem,
    recv_sem,
    load_sem,
    part_send,
    part_recv,
):
    count = length * PAIR
    total = count * cols
    block, width = hamil.shape
    row_blocks = product.shape[0] // block
    panels = width // block
    piece = block // CHUNKS
    me = lax.axis_index("blk")
    my_col = lax.axis_index("col")
    z = me // PAIR
    x = me % PAIR
    partner = me + 1 - 2 * x
    last = length - 1
    has_up = z < last
    has_down = z > 0

    loads = [
        pltpu.make_async_copy(source, target, load_sem.at[at])
        for at, (source, target) in enumerate(
            (
                (occ_hp_in, occ_hp),
                (window_in, window),
                (slab_in, slab),
                (groups_in, groups),
                (row_window_in, row_window),
                (occ_p_in, occ_p),
                (density, p_in),
            )
        )
    ]
    hamil_loads = [
        pltpu.make_async_copy(
            hamil_in.at[pl.ds(chunk * piece, piece)],
            hamil.at[pl.ds(chunk * piece, piece)],
            load_sem.at[len(loads) + chunk],
        )
        for chunk in range(CHUNKS)
    ]
    barrier = pltpu.get_barrier_semaphore()

    def greet(device):
        pl.semaphore_signal(barrier, inc=1, device_id=device, device_id_type=MESH)

    greet({"blk": partner})

    @pl.when(has_up)
    def _():
        greet({"blk": me + PAIR})

    @pl.when(has_down)
    def _():
        greet({"blk": me - PAIR})

    @pl.loop(1, cols)
    def greet_col(step):
        greet({"col": (my_col + step) % cols})

    for load in loads[:4] + hamil_loads + loads[4:]:
        load.start()

    for load in loads[:4]:
        load.wait()

    def move(where, k, chunk, device):
        rows = gathered.at[k, pl.ds(chunk * piece, piece), :]
        return pltpu.make_async_remote_copy(
            src_ref=rows,
            dst_ref=rows,
            send_sem=send_sem.at[where, k],
            recv_sem=recv_sem.at[k, chunk],
            device_id={"blk": device},
            device_id_type=MESH,
        )

    def wait_sent(where, k, first, chunks):
        rows = gathered.at[k, pl.ds(first * piece, chunks * piece), :]
        pltpu.make_async_copy(rows, rows, send_sem.at[where, k]).wait()

    def up(k, chunk):
        return move(0, k, chunk, me + PAIR)

    def down(k, chunk):
        return move(1, k, chunk, me - PAIR)

    def across(k, chunk):
        return move(2, k, chunk, partner)

    piece_row = lax.broadcasted_iota(jnp.int32, (piece, block), 0)
    piece_col = lax.broadcasted_iota(jnp.int32, (piece, block), 1)
    order = list(range(EXTRA, CHUNKS)) + list(range(EXTRA))
    for at, chunk in enumerate(order):
        hamil_loads[chunk].wait()
        there = pl.ds(chunk * piece, piece)
        rows_live = piece_row + chunk * piece < window[me]
        for panel in range(panels):
            size = groups[slab[panel]]
            occupied = occ_hp[0, panel].astype(jnp.float32)
            mask = jnp.where(rows_live & (piece_col < size), occupied, 0.0)
            here = pl.ds(panel * block, block)
            gathered[me, there, here] = hamil[there, here] * mask
        if at == 0:
            ends = jnp.int32(z == 0) + jnp.int32(z == last)
            pl.semaphore_wait(barrier, PAIR - 1 + cols - 1 + 2 - ends)

        across(me, chunk).start()

        @pl.when(has_up)
        def _():
            up(me, chunk).start()

        @pl.when(has_down)
        def _():
            down(me, chunk).start()

    for load in loads[4:]:
        load.wait()

    row_at = lax.broadcasted_iota(jnp.int32, (block, block), 0)
    col_at = lax.broadcasted_iota(jnp.int32, (block, block), 1)

    @pl.loop(0, length)
    def split(at):
        for b in range(row_blocks):
            live = row_at < row_window[me * row_blocks + b]
            here = pl.ds(b * block, block)
            for other in range(PAIR):
                k = at * PAIR + other
                mask = jnp.where(
                    live & (col_at < window[k]), occ_p[b, k].astype(jnp.float32), 0.0
                )
                value = p_in[here, pl.ds(pl.multiple_of(k * block, block), block)] * mask
                high = value.astype(jnp.bfloat16)
                there = pl.ds(other * block, block)
                p_high[at, here, there] = high
                p_low[at, here, there] = (value - high.astype(jnp.float32)).astype(jnp.bfloat16)

    def times(a, b):
        return jnp.dot(a, b, preferred_element_type=jnp.float32)

    def pass_line(distance):
        @pl.loop(0, CHUNKS)
        def each(step):
            chunk = (step + EXTRA) % CHUNKS

            @pl.when(z - distance >= 0)
            def _():
                k = me - distance * PAIR
                across(k, chunk).wait_recv()

                @pl.when(has_up)
                def _():
                    up(k, chunk).start()

                @pl.when((z != distance) | (chunk >= EXTRA))
                def _():
                    across(k, chunk).start()

            @pl.when(z + distance < length)
            def _():
                k = me + distance * PAIR
                across(k, chunk).wait_recv()

                @pl.when(has_down)
                def _():
                    down(k, chunk).start()

                @pl.when((z + distance != last) | (chunk >= EXTRA))
                def _():
                    across(k, chunk).start()

    def pass_ends(distance):
        @pl.loop(0, EXTRA)
        def each(chunk):
            @pl.when(z == distance)
            def _():
                k = 1 - x
                across(k, chunk).wait_recv()

                @pl.when(has_up)
                def _():
                    up(k, chunk).start()

            if length > 1:

                @pl.when(z + distance == last)
                def _():
                    k = last * PAIR + 1 - x
                    across(k, chunk).wait_recv()

                    @pl.when(has_down)
                    def _():
                        down(k, chunk).start()

    def sends_done():
        @pl.loop(0, length)
        def sent(at):
            k = at * PAIR + x
            end = ((at == 0) | (at == last)) & (at != z)

            @pl.when(has_up & (at <= z))
            def _():
                wait_sent(0, k, 0, CHUNKS)

            @pl.when(has_down & (at >= z))
            def _():
                wait_sent(1, k, 0, CHUNKS)

            @pl.when(end)
            def _():
                wait_sent(2, k, EXTRA, CHUNKS - EXTRA)

            @pl.when(jnp.logical_not(end))
            def _():
                wait_sent(2, k, 0, CHUNKS)

        @pl.when(has_up)
        def _():
            wait_sent(0, 1 - x, 0, EXTRA)

        @pl.when(has_down)
        def _():
            wait_sent(1, last * PAIR + 1 - x, 0, EXTRA)

    def add_terms(distance):
        @pl.loop(0, 2)
        def each(way):
            at = z + (2 * way - 1) * distance

            @pl.when((at >= 0) & (at < length) & ((distance > 0) | (way > 0)))
            def _():
                end = jnp.int32((at == 0) | (at == last))

                @pl.loop(EXTRA * end, CHUNKS)
                def wait(chunk):
                    across(at * PAIR + 1 - x, chunk).wait_recv()

                left_high = p_high[at]
                left_low = p_low[at]

                @pl.loop(0, width // half)
                def columns(part):
                    here = pl.ds(pl.multiple_of(part * half, half), half)
                    right = gathered[pl.ds(at * PAIR, PAIR), :, here].reshape(PAIR * block, half)
                    high = right.astype(jnp.bfloat16)
                    low = (right - high.astype(jnp.float32)).astype(jnp.bfloat16)
                    value = times(left_high, low) + times(left_low, high) + times(left_high, high)
                    product[:, here] = product[:, here] + value

    half = HALF
    product[...] = jnp.zeros_like(product)

    @pl.loop(1, length + 1)
    def steps(distance):
        pass_line(distance)
        pass_ends(distance - 1)

        @pl.when(distance == length)
        def _():
            sends_done()

        add_terms(distance - 1)

    lane = 128
    squares = product[...] * product[...]
    squares = jnp.sum(squares.reshape(squares.shape[0] // 8, 8, width), axis=0)
    mine = squares[:, :lane]
    for panel in range(1, width // lane):
        mine = mine + squares[:, panel * lane : (panel + 1) * lane]
    spot = me * cols + my_col
    parts[spot, 0:1] = jnp.sum(mine, axis=0, keepdims=True)

    def part(slot, device):
        return pltpu.make_async_remote_copy(
            src_ref=parts.at[slot, pl.ds(0, 1)],
            dst_ref=parts.at[slot, pl.ds(0, 1)],
            send_sem=part_send.at[device],
            recv_sem=part_recv.at[slot],
            device_id={"blk": device // cols, "col": device % cols},
            device_id_type=MESH,
        )

    @pl.loop(1, total)
    def send_parts(step):
        part(spot, (spot + step) % total).start()

    @pl.loop(1, total)
    def get_parts(step):
        other = (spot + step) % total
        part(other, other).wait_recv()

    norm[0] = jnp.sum(parts[:, 0, :])

    @pl.loop(1, total)
    def sent_parts(step):
        part(spot, (spot + step) % total).wait_send()


def finish(product_in, norm_in, product_out, norm_out, sem):
    store = pltpu.make_async_copy(product_in, product_out, sem)
    store.start()
    norm_out[0] = norm_in[0]
    store.wait()


def solution(mesh):
    count = mesh.shape["blk"]
    cols = mesh.shape["col"]
    length = count // PAIR

    def per_device(
        density,
        occupied_p,
        hamil_dens,
        occupied_hp,
        window_sizes,
        row_window_sizes,
        slab_index,
        group_sizes,
    ):
        rows, inner = density.shape
        block, width = hamil_dens.shape
        hbm = pl.BlockSpec(memory_space=pltpu.HBM)
        vmem = pl.BlockSpec(memory_space=pltpu.VMEM)
        smem = pl.BlockSpec(memory_space=pltpu.SMEM)
        product, norm = pl.pallas_call(
            functools.partial(kernel, length, cols),
            out_shape=(
                pltpu.VMEM((rows, width), jnp.float32),
                jax.ShapeDtypeStruct((1,), jnp.float32),
            ),
            in_specs=[hbm] * 8,
            out_specs=(vmem, smem),
            scratch_shapes=[
                pltpu.VMEM((block, width), jnp.float32),
                pltpu.SMEM(occupied_p.shape, jnp.int32),
                pltpu.SMEM(occupied_hp.shape, jnp.int32),
                pltpu.SMEM(window_sizes.shape, jnp.int32),
                pltpu.SMEM(row_window_sizes.shape, jnp.int32),
                pltpu.SMEM(slab_index.shape, jnp.int32),
                pltpu.SMEM(group_sizes.shape, jnp.int32),
                pltpu.VMEM((count, block, width), jnp.float32),
                pltpu.VMEM((rows, inner), jnp.float32),
                pltpu.VMEM((length, rows, PAIR * block), jnp.bfloat16),
                pltpu.VMEM((length, rows, PAIR * block), jnp.bfloat16),
                pltpu.VMEM((count * cols, 8, 128), jnp.float32),
                pltpu.SemaphoreType.DMA((3, count)),
                pltpu.SemaphoreType.DMA((count, CHUNKS)),
                pltpu.SemaphoreType.DMA((7 + CHUNKS,)),
                pltpu.SemaphoreType.DMA((count * cols,)),
                pltpu.SemaphoreType.DMA((count * cols,)),
            ],
            compiler_params=pltpu.CompilerParams(
                collective_id=0, has_side_effects=True, vmem_limit_bytes=56 << 20
            ),
        )(
            *(
                pltpu.with_memory_space_constraint(value, pltpu.HBM)
                for value in (
                    density,
                    hamil_dens,
                    occupied_p,
                    occupied_hp,
                    window_sizes,
                    row_window_sizes,
                    slab_index,
                    group_sizes,
                )
            )
        )
        product, norm = pl.pallas_call(
            finish,
            out_shape=(
                jax.ShapeDtypeStruct((rows, width), jnp.float32),
                jax.ShapeDtypeStruct((1,), jnp.float32),
            ),
            in_specs=[vmem, smem],
            out_specs=(hbm, smem),
            scratch_shapes=[pltpu.SemaphoreType.DMA(())],
            compiler_params=pltpu.CompilerParams(vmem_limit_bytes=1 << 20),
        )(pltpu.with_memory_space_constraint(product, pltpu.VMEM), norm)
        return product, norm.reshape(())

    return jax.shard_map(
        per_device,
        mesh=mesh,
        in_specs=(
            P("blk", None),
            P("blk", None),
            P("blk", "col"),
            P("blk", "col"),
            P(),
            P(),
            P("col"),
            P(),
        ),
        out_specs=(P("blk", "col"), P()),
        check_vma=False,
    )
```

```python
import functools

import jax
import jax.numpy as jnp
from jax import lax
from jax.experimental import pallas as pl
from jax.experimental.pallas import tpu as pltpu
from jax.sharding import PartitionSpec as P

MESH = pl.DeviceIdType.MESH
PAIR = 2
CHUNKS = 4
EXTRA = 2
HALF = 512


def kernel(
    length,
    cols,
    density,
    hamil_in,
    occ_p_in,
    occ_hp_in,
    window_in,
    row_window_in,
    slab_in,
    groups_in,
    product,
    norm,
    hamil,
    occ_p,
    occ_hp,
    window,
    row_window,
    slab,
    groups,
    gathered,
    p_in,
    p_high,
    p_low,
    parts,
    send_sem,
    recv_sem,
    load_sem,
    part_send,
    part_recv,
):
    count = length * PAIR
    total = count * cols
    block, width = hamil.shape
    row_blocks = product.shape[0] // block
    panels = width // block
    piece = block // CHUNKS
    me = lax.axis_index("blk")
    my_col = lax.axis_index("col")
    z = me // PAIR
    x = me % PAIR
    partner = me + 1 - 2 * x
    last = length - 1
    has_up = z < last
    has_down = z > 0

    loads = [
        pltpu.make_async_copy(source, target, load_sem.at[at])
        for at, (source, target) in enumerate(
            (
                (occ_hp_in, occ_hp),
                (window_in, window),
                (slab_in, slab),
                (groups_in, groups),
                (row_window_in, row_window),
                (occ_p_in, occ_p),
                (density, p_in),
            )
        )
    ]
    hamil_loads = [
        pltpu.make_async_copy(
            hamil_in.at[pl.ds(chunk * piece, piece)],
            hamil.at[pl.ds(chunk * piece, piece)],
            load_sem.at[len(loads) + chunk],
        )
        for chunk in range(CHUNKS)
    ]
    barrier = pltpu.get_barrier_semaphore()

    def greet(device):
        pl.semaphore_signal(barrier, inc=1, device_id=device, device_id_type=MESH)

    greet({"blk": partner})

    @pl.when(has_up)
    def _():
        greet({"blk": me + PAIR})

    @pl.when(has_down)
    def _():
        greet({"blk": me - PAIR})

    @pl.loop(1, cols)
    def greet_col(step):
        greet({"col": (my_col + step) % cols})

    for load in loads[:4] + hamil_loads + loads[4:]:
        load.start()

    for load in loads[:4]:
        load.wait()

    def move(where, k, chunk, device):
        rows = gathered.at[k, pl.ds(chunk * piece, piece), :]
        return pltpu.make_async_remote_copy(
            src_ref=rows,
            dst_ref=rows,
            send_sem=send_sem.at[where, k],
            recv_sem=recv_sem.at[k, chunk],
            device_id={"blk": device},
            device_id_type=MESH,
        )

    def wait_sent(where, k, first, chunks):
        rows = gathered.at[k, pl.ds(first * piece, chunks * piece), :]
        pltpu.make_async_copy(rows, rows, send_sem.at[where, k]).wait()

    def up(k, chunk):
        return move(0, k, chunk, me + PAIR)

    def down(k, chunk):
        return move(1, k, chunk, me - PAIR)

    def across(k, chunk):
        return move(2, k, chunk, partner)

    piece_row = lax.broadcasted_iota(jnp.int32, (piece, block), 0)
    piece_col = lax.broadcasted_iota(jnp.int32, (piece, block), 1)
    order = list(range(EXTRA, CHUNKS)) + list(range(EXTRA))
    for at, chunk in enumerate(order):
        hamil_loads[chunk].wait()
        there = pl.ds(chunk * piece, piece)
        rows_live = piece_row + chunk * piece < window[me]
        for panel in range(panels):
            size = groups[slab[panel]]
            occupied = occ_hp[0, panel].astype(jnp.float32)
            mask = jnp.where(rows_live & (piece_col < size), occupied, 0.0)
            here = pl.ds(panel * block, block)
            gathered[me, there, here] = hamil[there, here] * mask
        if at == 0:
            ends = jnp.int32(z == 0) + jnp.int32(z == last)
            pl.semaphore_wait(barrier, PAIR - 1 + cols - 1 + 2 - ends)

        across(me, chunk).start()

        @pl.when(has_up)
        def _():
            up(me, chunk).start()

        @pl.when(has_down)
        def _():
            down(me, chunk).start()

    for load in loads[4:]:
        load.wait()

    row_at = lax.broadcasted_iota(jnp.int32, (block, block), 0)
    col_at = lax.broadcasted_iota(jnp.int32, (block, block), 1)

    @pl.loop(0, length)
    def split(at):
        for b in range(row_blocks):
            live = row_at < row_window[me * row_blocks + b]
            here = pl.ds(b * block, block)
            for other in range(PAIR):
                k = at * PAIR + other
                mask = jnp.where(
                    live & (col_at < window[k]), occ_p[b, k].astype(jnp.float32), 0.0
                )
                value = p_in[here, pl.ds(pl.multiple_of(k * block, block), block)] * mask
                high = value.astype(jnp.bfloat16)
                there = pl.ds(other * block, block)
                p_high[at, here, there] = high
                p_low[at, here, there] = (value - high.astype(jnp.float32)).astype(jnp.bfloat16)

    def times(a, b):
        return jnp.dot(a, b, preferred_element_type=jnp.float32)

    def pass_line(distance):
        @pl.loop(0, CHUNKS)
        def each(step):
            chunk = (step + EXTRA) % CHUNKS

            @pl.when(z - distance >= 0)
            def _():
                k = me - distance * PAIR
                across(k, chunk).wait_recv()

                @pl.when(has_up)
                def _():
                    up(k, chunk).start()

                @pl.when((z != distance) | (chunk >= EXTRA))
                def _():
                    across(k, chunk).start()

            @pl.when(z + distance < length)
            def _():
                k = me + distance * PAIR
                across(k, chunk).wait_recv()

                @pl.when(has_down)
                def _():
                    down(k, chunk).start()

                @pl.when((z + distance != last) | (chunk >= EXTRA))
                def _():
                    across(k, chunk).start()

    def pass_ends(distance):
        @pl.loop(0, EXTRA)
        def each(chunk):
            @pl.when(z == distance)
            def _():
                k = 1 - x
                across(k, chunk).wait_recv()

                @pl.when(has_up)
                def _():
                    up(k, chunk).start()

            if length > 1:

                @pl.when(z + distance == last)
                def _():
                    k = last * PAIR + 1 - x
                    across(k, chunk).wait_recv()

                    @pl.when(has_down)
                    def _():
                        down(k, chunk).start()

    def sends_done():
        @pl.loop(0, length)
        def sent(at):
            k = at * PAIR + x
            end = ((at == 0) | (at == last)) & (at != z)

            @pl.when(has_up & (at <= z))
            def _():
                wait_sent(0, k, 0, CHUNKS)

            @pl.when(has_down & (at >= z))
            def _():
                wait_sent(1, k, 0, CHUNKS)

            @pl.when(end)
            def _():
                wait_sent(2, k, EXTRA, CHUNKS - EXTRA)

            @pl.when(jnp.logical_not(end))
            def _():
                wait_sent(2, k, 0, CHUNKS)

        @pl.when(has_up)
        def _():
            wait_sent(0, 1 - x, 0, EXTRA)

        @pl.when(has_down)
        def _():
            wait_sent(1, last * PAIR + 1 - x, 0, EXTRA)

    def add_terms(distance):
        @pl.loop(0, 2)
        def each(way):
            at = z + (2 * way - 1) * distance

            @pl.when((at >= 0) & (at < length) & ((distance > 0) | (way > 0)))
            def _():
                end = jnp.int32((at == 0) | (at == last))

                @pl.loop(EXTRA * end, CHUNKS)
                def wait(chunk):
                    across(at * PAIR + 1 - x, chunk).wait_recv()

                left_high = p_high[at]
                left_low = p_low[at]

                @pl.loop(0, width // half)
                def columns(part):
                    here = pl.ds(pl.multiple_of(part * half, half), half)
                    right = gathered[pl.ds(at * PAIR, PAIR), :, here].reshape(PAIR * block, half)
                    high = right.astype(jnp.bfloat16)
                    low = (right - high.astype(jnp.float32)).astype(jnp.bfloat16)
                    value = times(left_high, low) + times(left_low, high) + times(left_high, high)
                    product[:, here] = product[:, here] + value

    half = HALF
    product[...] = jnp.zeros_like(product)

    @pl.loop(1, length + 1)
    def steps(distance):
        pass_line(distance)
        pass_ends(distance - 1)

        @pl.when(distance == length)
        def _():
            sends_done()

        add_terms(distance - 1)

    lane = 128
    squares = product[...] * product[...]
    squares = jnp.sum(squares.reshape(squares.shape[0] // 8, 8, width), axis=0)
    mine = squares[:, :lane]
    for panel in range(1, width // lane):
        mine = mine + squares[:, panel * lane : (panel + 1) * lane]
    spot = me * cols + my_col
    parts[spot, 0:1] = jnp.sum(mine, axis=0, keepdims=True)

    def part(slot, device):
        return pltpu.make_async_remote_copy(
            src_ref=parts.at[slot, pl.ds(0, 1)],
            dst_ref=parts.at[slot, pl.ds(0, 1)],
            send_sem=part_send.at[device],
            recv_sem=part_recv.at[slot],
            device_id={"blk": device // cols, "col": device % cols},
            device_id_type=MESH,
        )

    @pl.loop(1, total)
    def send_parts(step):
        part(spot, (spot + step) % total).start()

    @pl.loop(1, total)
    def get_parts(step):
        other = (spot + step) % total
        part(other, other).wait_recv()

    norm[...] = jnp.sum(parts[:, 0, :], axis=0, keepdims=True)

    @pl.loop(1, total)
    def sent_parts(step):
        part(spot, (spot + step) % total).wait_send()


def finish(product_in, norm_in, product_out, norm_out, value, sem):
    store = pltpu.make_async_copy(product_in, product_out, sem.at[0])
    store.start()
    value[0] = jnp.sum(norm_in[...])
    send = pltpu.make_async_copy(value, norm_out, sem.at[1])
    send.start()
    store.wait()
    send.wait()


def solution(mesh):
    count = mesh.shape["blk"]
    cols = mesh.shape["col"]
    length = count // PAIR

    def per_device(
        density,
        occupied_p,
        hamil_dens,
        occupied_hp,
        window_sizes,
        row_window_sizes,
        slab_index,
        group_sizes,
    ):
        rows, inner = density.shape
        block, width = hamil_dens.shape
        hbm = pl.BlockSpec(memory_space=pltpu.HBM)
        vmem = pl.BlockSpec(memory_space=pltpu.VMEM)
        smem = pl.BlockSpec(memory_space=pltpu.SMEM)
        product, norm = pl.pallas_call(
            functools.partial(kernel, length, cols),
            out_shape=(
                pltpu.VMEM((rows, width), jnp.float32),
                pltpu.VMEM((1, 128), jnp.float32),
            ),
            in_specs=[hbm] * 8,
            out_specs=(vmem, vmem),
            scratch_shapes=[
                pltpu.VMEM((block, width), jnp.float32),
                pltpu.SMEM(occupied_p.shape, jnp.int32),
                pltpu.SMEM(occupied_hp.shape, jnp.int32),
                pltpu.SMEM(window_sizes.shape, jnp.int32),
                pltpu.SMEM(row_window_sizes.shape, jnp.int32),
                pltpu.SMEM(slab_index.shape, jnp.int32),
                pltpu.SMEM(group_sizes.shape, jnp.int32),
                pltpu.VMEM((count, block, width), jnp.float32),
                pltpu.VMEM((rows, inner), jnp.float32),
                pltpu.VMEM((length, rows, PAIR * block), jnp.bfloat16),
                pltpu.VMEM((length, rows, PAIR * block), jnp.bfloat16),
                pltpu.VMEM((count * cols, 8, 128), jnp.float32),
                pltpu.SemaphoreType.DMA((3, count)),
                pltpu.SemaphoreType.DMA((count, CHUNKS)),
                pltpu.SemaphoreType.DMA((7 + CHUNKS,)),
                pltpu.SemaphoreType.DMA((count * cols,)),
                pltpu.SemaphoreType.DMA((count * cols,)),
            ],
            compiler_params=pltpu.CompilerParams(
                collective_id=0, has_side_effects=True, vmem_limit_bytes=56 << 20
            ),
        )(
            *(
                pltpu.with_memory_space_constraint(value, pltpu.HBM)
                for value in (
                    density,
                    hamil_dens,
                    occupied_p,
                    occupied_hp,
                    window_sizes,
                    row_window_sizes,
                    slab_index,
                    group_sizes,
                )
            )
        )
        product, norm = pl.pallas_call(
            finish,
            out_shape=(
                jax.ShapeDtypeStruct((rows, width), jnp.float32),
                jax.ShapeDtypeStruct((1,), jnp.float32),
            ),
            in_specs=[vmem, vmem],
            out_specs=(hbm, hbm),
            scratch_shapes=[pltpu.SMEM((1,), jnp.float32), pltpu.SemaphoreType.DMA((2,))],
            compiler_params=pltpu.CompilerParams(vmem_limit_bytes=1 << 20),
        )(pltpu.with_memory_space_constraint(product, pltpu.VMEM), pltpu.with_memory_space_constraint(norm, pltpu.VMEM))
        return product, norm.reshape(())

    return jax.shard_map(
        per_device,
        mesh=mesh,
        in_specs=(
            P("blk", None),
            P("blk", None),
            P("blk", "col"),
            P("blk", "col"),
            P(),
            P(),
            P("col"),
            P(),
        ),
        out_specs=(P("blk", "col"), P()),
        check_vma=False,
    )
```

```python
import functools

import jax
import jax.numpy as jnp
from jax import lax
from jax.experimental import pallas as pl
from jax.experimental.pallas import tpu as pltpu
from jax.sharding import PartitionSpec as P

MESH = pl.DeviceIdType.MESH
PAIR = 2
EXTRA = 2
TOP_EXTRA = 1
NEAR = 2
CORES = 2
FAR_AFTER = 1


def kernel(
    length,
    cols,
    density,
    hamil_in,
    occ_p_in,
    occ_hp_in,
    window_in,
    row_window_in,
    slab_in,
    groups_in,
    product,
    norm,
    hamil,
    occ_p,
    occ_hp,
    window,
    row_window,
    slab,
    groups,
    gathered,
    p_in,
    p_high,
    p_low,
    p_far,
    far_part,
    parts,
    send_sem,
    recv_sem,
    load_sem,
    part_send,
    part_recv,
    far_send,
    far_recv,
    far_sem,
):
    count = length * PAIR
    total = count * cols
    block, width = hamil.shape
    row_blocks = product.shape[0] // block
    panels = width // block
    far = length >= NEAR + 2
    me = lax.axis_index("blk")
    my_col = lax.axis_index("col")
    z = me // PAIR
    x = me % PAIR
    partner = me + 1 - 2 * x
    last = length - 1
    has_up = z < last
    has_down = z > 0
    is_last = z == last
    is_near = z == last - 1

    loads = [
        pltpu.make_async_copy(source, target, load_sem.at[at])
        for at, (source, target) in enumerate(
            (
                (occ_hp_in, occ_hp),
                (window_in, window),
                (slab_in, slab),
                (groups_in, groups),
                (row_window_in, row_window),
                (occ_p_in, occ_p),
                (density, p_in),
            )
        )
    ]
    hamil_loads = [
        pltpu.make_async_copy(
            hamil_in.at[:, pl.ds(panel * block, block)],
            hamil.at[:, pl.ds(panel * block, block)],
            load_sem.at[len(loads) + panel],
        )
        for panel in range(panels)
    ]
    barrier = pltpu.get_barrier_semaphore()

    def greet(device):
        pl.semaphore_signal(barrier, inc=1, device_id=device, device_id_type=MESH)

    greet({"blk": partner})

    @pl.when(has_up)
    def _():
        greet({"blk": me + PAIR})

    @pl.when(has_down)
    def _():
        greet({"blk": me - PAIR})

    @pl.loop(1, cols)
    def greet_col(step):
        greet({"col": (my_col + step) % cols})

    for load in loads[:4] + hamil_loads + loads[4:]:
        load.start()

    for load in loads[:4]:
        load.wait()

    def move(where, k, panel, device):
        spot = gathered.at[k, panel]
        return pltpu.make_async_remote_copy(
            src_ref=spot,
            dst_ref=spot,
            send_sem=send_sem.at[where, k],
            recv_sem=recv_sem.at[k, panel],
            device_id={"blk": device},
            device_id_type=MESH,
        )

    def wait_sent(where, k, first, amount):
        spot = gathered.at[k, pl.ds(first, amount)]
        pltpu.make_async_copy(spot, spot, send_sem.at[where, k]).wait()

    def up(k, panel):
        return move(0, k, panel, me + PAIR)

    def down(k, panel):
        return move(1, k, panel, me - PAIR)

    def across(k, panel):
        return move(2, k, panel, partner)

    share = product.shape[0] // cols
    pair = PAIR * block

    mate = my_col + 1 - CORES * (my_col % CORES)

    def far_move(who, plane, device, sem, onward=0):
        spot = p_far.at[pl.ds(pl.multiple_of(who * share, share), share), pl.ds(plane * pair, pair)]
        return pltpu.make_async_remote_copy(
            src_ref=spot,
            dst_ref=spot,
            send_sem=far_send.at[onward, sem, plane],
            recv_sem=far_recv.at[who, plane],
            device_id=device,
            device_id_type=MESH,
        )

    def far_down(plane):
        return far_move(my_col, plane, {"blk": me - PAIR}, my_col)

    def far_to(peer, plane):
        return far_move(my_col, plane, {"col": peer}, peer)

    def far_result():
        return pltpu.make_async_remote_copy(
            src_ref=far_part,
            dst_ref=far_part,
            send_sem=far_sem.at[0],
            recv_sem=far_sem.at[1],
            device_id={"blk": me + PAIR},
            device_id_type=MESH,
        )

    row_at = lax.broadcasted_iota(jnp.int32, (block, block), 0)
    col_at = lax.broadcasted_iota(jnp.int32, (block, block), 1)

    def send_far():
        for load in loads[4:]:
            load.wait()
        first = my_col * share
        b = first // block
        share_row = lax.broadcasted_iota(jnp.int32, (share, block), 0) + first - b * block
        share_col = lax.broadcasted_iota(jnp.int32, (share, block), 1)
        rows = pl.ds(pl.multiple_of(first, share), share)
        live = share_row < row_window[me * row_blocks + b]
        for plane in range(NEAR):
            for other in range(PAIR):
                k = (last - NEAR + plane) * PAIR + other
                mask = jnp.where(
                    live & (share_col < window[k]), occ_p[b, k].astype(jnp.float32), 0.0
                )
                p_far[rows, pl.ds(plane * pair + other * block, block)] = (
                    p_in[rows, pl.ds(k * block, block)] * mask
                )
            far_down(plane).start()
        for plane in range(NEAR):
            for other in range(PAIR):
                k = (last - NEAR + plane) * PAIR + other
                gathered[k, 0] = jnp.zeros((block, block), jnp.float32)

    rows_live = row_at < window[me]
    for panel in range(panels):
        hamil_loads[panel].wait()
        size = groups[slab[panel]]
        occupied = occ_hp[0, panel].astype(jnp.float32)
        mask = jnp.where(rows_live & (col_at < size), occupied, 0.0)
        gathered[me, panel] = hamil[:, panel * block : (panel + 1) * block] * mask
        if panel == 0:
            ends = jnp.int32(z == 0) + jnp.int32(z == last)
            pl.semaphore_wait(barrier, PAIR - 1 + cols - 1 + 2 - ends)

        across(me, panel).start()
        if panel == 0 and far:

            @pl.when(has_up & jnp.logical_not(is_near))
            def _():
                up(me, panel).start()

        else:

            @pl.when(has_up)
            def _():
                up(me, panel).start()

        @pl.when(has_down)
        def _():
            down(me, panel).start()

        if panel == FAR_AFTER and far:
            pl.when(is_last)(send_far)

    def wait_loads():
        for load in loads[4:]:
            load.wait()

    if far:
        pl.when(jnp.logical_not(is_last))(wait_loads)
    else:
        wait_loads()

    @pl.loop(0, length)
    def split(at):
        for b in range(row_blocks):
            live = row_at < row_window[me * row_blocks + b]
            here = pl.ds(b * block, block)
            for other in range(PAIR):
                k = at * PAIR + other
                mask = jnp.where(
                    live & (col_at < window[k]), occ_p[b, k].astype(jnp.float32), 0.0
                )
                value = p_in[here, pl.ds(pl.multiple_of(k * block, block), block)] * mask
                high = value.astype(jnp.bfloat16)
                there = pl.ds(other * block, block)
                p_high[at, here, there] = high
                p_low[at, here, there] = (value - high.astype(jnp.float32)).astype(jnp.bfloat16)

    def times(a, b):
        return jnp.dot(a, b, preferred_element_type=jnp.float32)

    def first_panel(at):
        if not far:
            return 0
        return jnp.int32(is_last & (at >= last - NEAR) & (at < last))

    def end_panel(at):
        low = (at == 0) & (z > 0)
        high = (at == last) & (z < last)
        top = low & is_last
        return panels - EXTRA * jnp.int32(low | high) + (EXTRA - TOP_EXTRA) * jnp.int32(top)

    def pass_below(distance, panel):
        at = z - distance

        @pl.when((at >= 0) & (distance > 0) & (panel >= first_panel(at)))
        def _():
            k = me - distance * PAIR
            across(k, panel).wait_recv()
            skip = (panel == 0) & is_near & (at >= last - NEAR) if far else False

            @pl.when(has_up & jnp.logical_not(skip))
            def _():
                up(k, panel).start()

            @pl.when(panel < end_panel(at))
            def _():
                across(k, panel).start()

    def pass_above(distance, panel):
        at = z + distance

        @pl.when((at < length) & (distance > 0))
        def _():
            k = me + distance * PAIR
            across(k, panel).wait_recv()

            @pl.when(has_down)
            def _():
                down(k, panel).start()

            @pl.when(panel < end_panel(at))
            def _():
                across(k, panel).start()

    def pass_low_end(distance):
        @pl.when((z == distance) & has_up)
        def _():
            for panel in range(panels - EXTRA, panels):
                k = 1 - x
                across(k, panel).wait_recv()
                if panel >= panels - TOP_EXTRA:
                    up(k, panel).start()
                else:

                    @pl.when(jnp.logical_not(is_near))
                    def _():
                        up(k, panel).start()

    def pass_high_end(distance):
        @pl.when((z + distance == last) & has_down)
        def _():
            for panel in range(panels - EXTRA, panels):
                k = last * PAIR + 1 - x
                across(k, panel).wait_recv()
                down(k, panel).start()

    def sends_done():
        @pl.loop(0, length)
        def sent(at):
            k = at * PAIR + x

            @pl.when(has_down & (at >= z))
            def _():
                wait_sent(1, k, 0, panels)

            short = is_near & (at >= last - NEAR) if far else False

            @pl.when(has_up & (at <= z) & jnp.logical_not(short))
            def _():
                wait_sent(0, k, 0, panels)

            @pl.when(has_up & (at <= z) & short)
            def _():
                wait_sent(0, k, 1, panels - 1)

            amount = end_panel(at) - first_panel(at)
            for size in sorted({panels, panels - 1, panels - EXTRA, panels - TOP_EXTRA}):

                @pl.when(amount == size)
                def _():
                    wait_sent(2, k, 0, size)

        @pl.when(has_up & is_near)
        def _():
            wait_sent(0, 1 - x, 0, TOP_EXTRA)

        @pl.when(has_up & jnp.logical_not(is_near))
        def _():
            wait_sent(0, 1 - x, 0, EXTRA)

        @pl.when(has_down)
        def _():
            wait_sent(1, last * PAIR + 1 - x, 0, EXTRA)

        if far:

            @pl.when(is_last)
            def _():
                for plane in range(NEAR):
                    far_down(plane).wait_send()

            @pl.when(is_near)
            def _():
                @pl.loop(1, cols // CORES)
                def peers(step):
                    who = (my_col + step * CORES) % cols
                    for plane in range(NEAR):
                        far_to(who, plane).wait_send()
                        far_move(who, plane, {"col": mate}, who, 1).wait_send()

                for plane in range(NEAR):
                    far_to(mate, plane).wait_send()

                far_result().wait_send()

    def split_in_two(value):
        high = value.astype(jnp.bfloat16)
        return high, (value - high.astype(jnp.float32)).astype(jnp.bfloat16)

    def right_of(at, panel):
        return gathered[pl.ds(at * PAIR, PAIR), panel].reshape(pair, block)

    def add_terms(distance):
        @pl.loop(0, 2)
        def each(way):
            at = z + (2 * way - 1) * distance

            @pl.when((at >= 0) & (at < length) & ((distance > 0) | ((distance == 0) & (way > 0))))
            def _():
                passed = ((at == 0) & has_up) | ((at == last) & has_down)

                first = first_panel(at)
                if far:
                    first = first + jnp.int32(is_near & (at >= last - NEAR) & (at < last))

                @pl.loop(first, panels - EXTRA * jnp.int32(passed))
                def wait(panel):
                    across(at * PAIR + 1 - x, panel).wait_recv()

                if far:

                    @pl.when(is_last & (distance == last))
                    def _():
                        far_result().wait_recv()

                left_high = p_high[at]
                left_low = p_low[at]
                right = jnp.concatenate([right_of(at, panel) for panel in range(panels)], axis=1)
                high, low = split_in_two(right)
                value = times(left_high, low) + times(left_low, high) + times(left_high, high)
                product[...] = product[...] + value

    def forward_far(plane):
        far_to(mate, plane).wait_recv()

        @pl.loop(1, cols // CORES)
        def peers(step):
            far_to((my_col + step * CORES) % cols, plane).start()

        far_to(mate, plane).start()

    def mate_far(plane):
        @pl.loop(1, cols // CORES)
        def peers(step):
            who = (my_col + step * CORES) % cols
            far_move(who, plane, {"col": mate}, who, 1).wait_recv()
            far_move(who, plane, {"col": mate}, who, 1).start()

    def give_far():
        @pl.loop(0, cols // CORES)
        def mates(step):
            who = (mate + step * CORES) % cols
            for plane in range(NEAR):
                far_move(who, plane, {"col": mate}, who).wait_recv()

        value = None
        for plane in range(NEAR):
            at = last - NEAR + plane
            across(at * PAIR + 1 - x, 0).wait_recv()
            left_high, left_low = split_in_two(p_far[:, plane * pair : (plane + 1) * pair])
            high, low = split_in_two(right_of(at, 0))
            one = times(left_high, low) + times(left_low, high) + times(left_high, high)
            value = one if value is None else value + one
        far_part[...] = value
        far_result().start()

    product[...] = jnp.zeros_like(product)
    inner = jnp.int32((z > 0) & (z < last))

    @pl.loop(0, length + 2)
    def steps(distance):
        @pl.loop(0, panels)
        def lines(panel):
            pass_below(distance + 1, panel)
            ahead = distance * panels + panel + panels // 2
            pass_above(ahead // panels, ahead % panels)

        if far:

            @pl.when(is_near & (distance == 0))
            def _():
                for plane in range(NEAR):
                    forward_far(plane)

            @pl.when(is_near & (distance == 1))
            def _():
                for plane in range(NEAR):
                    mate_far(plane)

        pass_low_end(distance)
        pass_high_end(distance)
        if far:

            @pl.when(is_near & (distance == 1))
            def _():
                give_far()

        @pl.when(distance == length)
        def _():
            sends_done()

        add_terms(distance - 1 - inner)

    if far:

        @pl.when(is_last)
        def _():
            product[:, 0:block] = product[:, 0:block] + far_part[...]

    lane = 128
    squares = product[...] * product[...]
    squares = jnp.sum(squares.reshape(squares.shape[0] // 8, 8, width), axis=0)
    mine = squares[:, :lane]
    for panel in range(1, width // lane):
        mine = mine + squares[:, panel * lane : (panel + 1) * lane]
    spot = me * cols + my_col
    parts[spot, 0:1] = jnp.sum(mine, axis=0, keepdims=True)

    def part(slot, device):
        return pltpu.make_async_remote_copy(
            src_ref=parts.at[slot, pl.ds(0, 1)],
            dst_ref=parts.at[slot, pl.ds(0, 1)],
            send_sem=part_send.at[device],
            recv_sem=part_recv.at[slot],
            device_id={"blk": device // cols, "col": device % cols},
            device_id_type=MESH,
        )

    @pl.loop(0, total)
    def send_parts(device):
        @pl.when(device != spot)
        def _():
            part(spot, device).start()

    @pl.loop(1, total)
    def get_parts(step):
        other = (spot + step) % total
        part(other, other).wait_recv()

    norm[...] = jnp.sum(parts[:, 0, :], axis=0, keepdims=True)

    @pl.loop(1, total)
    def sent_parts(step):
        part(spot, (spot + step) % total).wait_send()


def finish(product_in, norm_in, product_out, norm_out, value, sem):
    store = pltpu.make_async_copy(product_in, product_out, sem.at[0])
    store.start()
    value[0] = jnp.sum(norm_in[...])
    send = pltpu.make_async_copy(value, norm_out, sem.at[1])
    send.start()
    store.wait()
    send.wait()


def solution(mesh):
    count = mesh.shape["blk"]
    cols = mesh.shape["col"]
    length = count // PAIR

    def per_device(
        density,
        occupied_p,
        hamil_dens,
        occupied_hp,
        window_sizes,
        row_window_sizes,
        slab_index,
        group_sizes,
    ):
        rows, inner = density.shape
        block, width = hamil_dens.shape
        hbm = pl.BlockSpec(memory_space=pltpu.HBM)
        vmem = pl.BlockSpec(memory_space=pltpu.VMEM)
        smem = pl.BlockSpec(memory_space=pltpu.SMEM)
        product, norm = pl.pallas_call(
            functools.partial(kernel, length, cols),
            out_shape=(
                pltpu.VMEM((rows, width), jnp.float32),
                pltpu.VMEM((1, 128), jnp.float32),
            ),
            in_specs=[hbm] * 8,
            out_specs=(vmem, vmem),
            scratch_shapes=[
                pltpu.VMEM((block, width), jnp.float32),
                pltpu.SMEM(occupied_p.shape, jnp.int32),
                pltpu.SMEM(occupied_hp.shape, jnp.int32),
                pltpu.SMEM(window_sizes.shape, jnp.int32),
                pltpu.SMEM(row_window_sizes.shape, jnp.int32),
                pltpu.SMEM(slab_index.shape, jnp.int32),
                pltpu.SMEM(group_sizes.shape, jnp.int32),
                pltpu.VMEM((count, width // block, block, block), jnp.float32),
                pltpu.VMEM((rows, inner), jnp.float32),
                pltpu.VMEM((length, rows, PAIR * block), jnp.bfloat16),
                pltpu.VMEM((length, rows, PAIR * block), jnp.bfloat16),
                pltpu.VMEM((rows, NEAR * PAIR * block), jnp.float32),
                pltpu.VMEM((rows, block), jnp.float32),
                pltpu.VMEM((count * cols, 8, 128), jnp.float32),
                pltpu.SemaphoreType.DMA((3, count)),
                pltpu.SemaphoreType.DMA((count, width // block)),
                pltpu.SemaphoreType.DMA((7 + width // block,)),
                pltpu.SemaphoreType.DMA((count * cols,)),
                pltpu.SemaphoreType.DMA((count * cols,)),
                pltpu.SemaphoreType.DMA((2, cols, NEAR)),
                pltpu.SemaphoreType.DMA((cols, NEAR)),
                pltpu.SemaphoreType.DMA((2,)),
            ],
            compiler_params=pltpu.CompilerParams(
                collective_id=0, has_side_effects=True, vmem_limit_bytes=56 << 20
            ),
        )(
            *(
                pltpu.with_memory_space_constraint(value, pltpu.HBM)
                for value in (
                    density,
                    hamil_dens,
                    occupied_p,
                    occupied_hp,
                    window_sizes,
                    row_window_sizes,
                    slab_index,
                    group_sizes,
                )
            )
        )
        product, norm = pl.pallas_call(
            finish,
            out_shape=(
                jax.ShapeDtypeStruct((rows, width), jnp.float32),
                jax.ShapeDtypeStruct((1,), jnp.float32),
            ),
            in_specs=[vmem, vmem],
            out_specs=(hbm, hbm),
            scratch_shapes=[pltpu.SMEM((1,), jnp.float32), pltpu.SemaphoreType.DMA((2,))],
            compiler_params=pltpu.CompilerParams(vmem_limit_bytes=1 << 20),
        )(pltpu.with_memory_space_constraint(product, pltpu.VMEM), pltpu.with_memory_space_constraint(norm, pltpu.VMEM))
        return product, norm.reshape(())

    return jax.shard_map(
        per_device,
        mesh=mesh,
        in_specs=(
            P("blk", None),
            P("blk", None),
            P("blk", "col"),
            P("blk", "col"),
            P(),
            P(),
            P("col"),
            P(),
        ),
        out_specs=(P("blk", "col"), P()),
        check_vma=False,
    )
```

```python
import functools

import jax
import jax.numpy as jnp
from jax import lax
from jax.experimental import pallas as pl
from jax.experimental.pallas import tpu as pltpu
from jax.sharding import PartitionSpec as P

MESH = pl.DeviceIdType.MESH
PAIR = 2
EXTRA = 2
TOP_EXTRA = 1
NEAR = 2
CORES = 2
GROUP = 2
FAR_AFTER = 1


def kernel(
    length,
    cols,
    density,
    hamil_in,
    occ_p_in,
    occ_hp_in,
    window_in,
    row_window_in,
    slab_in,
    groups_in,
    product,
    norm,
    hamil,
    occ_p,
    occ_hp,
    window,
    row_window,
    slab,
    groups,
    gathered,
    p_in,
    p_high,
    p_low,
    p_far,
    far_part,
    parts,
    send_sem,
    recv_sem,
    load_sem,
    part_sem,
    far_send,
    far_recv,
    far_sem,
):
    count = length * PAIR
    total = count * cols
    block, width = hamil.shape
    row_blocks = product.shape[0] // block
    panels = width // block
    far = length >= NEAR + 2
    me = lax.axis_index("blk")
    my_col = lax.axis_index("col")
    z = me // PAIR
    x = me % PAIR
    partner = me + 1 - 2 * x
    last = length - 1
    has_up = z < last
    has_down = z > 0
    is_last = z == last
    is_near = z == last - 1

    loads = [
        pltpu.make_async_copy(source, target, load_sem.at[at])
        for at, (source, target) in enumerate(
            (
                (occ_hp_in, occ_hp),
                (window_in, window),
                (slab_in, slab),
                (groups_in, groups),
                (row_window_in, row_window),
                (occ_p_in, occ_p),
                (density, p_in),
            )
        )
    ]
    hamil_loads = [
        pltpu.make_async_copy(
            hamil_in.at[:, pl.ds(panel * block, block)],
            hamil.at[:, pl.ds(panel * block, block)],
            load_sem.at[len(loads) + panel],
        )
        for panel in range(panels)
    ]
    barrier = pltpu.get_barrier_semaphore()

    def greet(device):
        pl.semaphore_signal(barrier, inc=1, device_id=device, device_id_type=MESH)

    greet({"blk": partner})

    @pl.when(has_up)
    def _():
        greet({"blk": me + PAIR})

    @pl.when(has_down)
    def _():
        greet({"blk": me - PAIR})

    @pl.loop(1, cols)
    def greet_col(step):
        greet({"col": (my_col + step) % cols})

    for load in loads[:4] + hamil_loads + loads[4:]:
        load.start()

    for load in loads[:4]:
        load.wait()

    def move(where, k, panel, device):
        spot = gathered.at[k, panel]
        return pltpu.make_async_remote_copy(
            src_ref=spot,
            dst_ref=spot,
            send_sem=send_sem.at[where, k],
            recv_sem=recv_sem.at[k, panel],
            device_id={"blk": device},
            device_id_type=MESH,
        )

    def wait_sent(where, k, first, amount):
        spot = gathered.at[k, pl.ds(first, amount)]
        pltpu.make_async_copy(spot, spot, send_sem.at[where, k]).wait()

    def up(k, panel):
        return move(0, k, panel, me + PAIR)

    def down(k, panel):
        return move(1, k, panel, me - PAIR)

    def across(k, panel):
        return move(2, k, panel, partner)

    share = product.shape[0] // cols
    pair = PAIR * block

    mate = my_col + 1 - CORES * (my_col % CORES)

    def far_move(who, plane, device, sem, onward=0):
        spot = p_far.at[pl.ds(pl.multiple_of(who * share, share), share), pl.ds(plane * pair, pair)]
        return pltpu.make_async_remote_copy(
            src_ref=spot,
            dst_ref=spot,
            send_sem=far_send.at[onward, sem, plane],
            recv_sem=far_recv.at[who, plane],
            device_id=device,
            device_id_type=MESH,
        )

    def far_down(plane):
        return far_move(my_col, plane, {"blk": me - PAIR}, my_col)

    def far_to(peer, plane):
        return far_move(my_col, plane, {"col": peer}, peer)

    def far_result():
        return pltpu.make_async_remote_copy(
            src_ref=far_part,
            dst_ref=far_part,
            send_sem=far_sem.at[0],
            recv_sem=far_sem.at[1],
            device_id={"blk": me + PAIR},
            device_id_type=MESH,
        )

    row_at = lax.broadcasted_iota(jnp.int32, (block, block), 0)
    col_at = lax.broadcasted_iota(jnp.int32, (block, block), 1)

    def send_far():
        for load in loads[4:]:
            load.wait()
        first = my_col * share
        b = first // block
        share_row = lax.broadcasted_iota(jnp.int32, (share, block), 0) + first - b * block
        share_col = lax.broadcasted_iota(jnp.int32, (share, block), 1)
        rows = pl.ds(pl.multiple_of(first, share), share)
        live = share_row < row_window[me * row_blocks + b]
        for plane in range(NEAR):
            for other in range(PAIR):
                k = (last - NEAR + plane) * PAIR + other
                mask = jnp.where(
                    live & (share_col < window[k]), occ_p[b, k].astype(jnp.float32), 0.0
                )
                p_far[rows, pl.ds(plane * pair + other * block, block)] = (
                    p_in[rows, pl.ds(k * block, block)] * mask
                )
            far_down(plane).start()
        for plane in range(NEAR):
            for other in range(PAIR):
                k = (last - NEAR + plane) * PAIR + other
                gathered[k, 0] = jnp.zeros((block, block), jnp.float32)

    rows_live = row_at < window[me]
    for panel in range(panels):
        hamil_loads[panel].wait()
        size = groups[slab[panel]]
        occupied = occ_hp[0, panel].astype(jnp.float32)
        mask = jnp.where(rows_live & (col_at < size), occupied, 0.0)
        gathered[me, panel] = hamil[:, panel * block : (panel + 1) * block] * mask
        if panel == 0:
            ends = jnp.int32(z == 0) + jnp.int32(z == last)
            pl.semaphore_wait(barrier, PAIR - 1 + cols - 1 + 2 - ends)

        across(me, panel).start()
        if panel == 0 and far:

            @pl.when(has_up & jnp.logical_not(is_near))
            def _():
                up(me, panel).start()

        else:

            @pl.when(has_up)
            def _():
                up(me, panel).start()

        @pl.when(has_down)
        def _():
            down(me, panel).start()

        if panel == FAR_AFTER and far:
            pl.when(is_last)(send_far)

    def wait_loads():
        for load in loads[4:]:
            load.wait()

    if far:
        pl.when(jnp.logical_not(is_last))(wait_loads)
    else:
        wait_loads()

    @pl.loop(0, length)
    def split(at):
        for b in range(row_blocks):
            live = row_at < row_window[me * row_blocks + b]
            here = pl.ds(b * block, block)
            for other in range(PAIR):
                k = at * PAIR + other
                mask = jnp.where(
                    live & (col_at < window[k]), occ_p[b, k].astype(jnp.float32), 0.0
                )
                value = p_in[here, pl.ds(pl.multiple_of(k * block, block), block)] * mask
                high = value.astype(jnp.bfloat16)
                there = pl.ds(other * block, block)
                p_high[at, here, there] = high
                p_low[at, here, there] = (value - high.astype(jnp.float32)).astype(jnp.bfloat16)

    def times(a, b):
        return jnp.dot(a, b, preferred_element_type=jnp.float32)

    def first_panel(at):
        if not far:
            return 0
        return jnp.int32(is_last & (at >= last - NEAR) & (at < last))

    def end_panel(at):
        low = (at == 0) & (z > 0)
        high = (at == last) & (z < last)
        top = low & is_last
        return panels - EXTRA * jnp.int32(low | high) + (EXTRA - TOP_EXTRA) * jnp.int32(top)

    def pass_below(distance, panel):
        at = z - distance

        @pl.when((at >= 0) & (distance > 0) & (panel >= first_panel(at)))
        def _():
            k = me - distance * PAIR
            across(k, panel).wait_recv()
            skip = (panel == 0) & is_near & (at >= last - NEAR) if far else False

            @pl.when(has_up & jnp.logical_not(skip))
            def _():
                up(k, panel).start()

            @pl.when(panel < end_panel(at))
            def _():
                across(k, panel).start()

    def pass_above(distance, panel):
        at = z + distance

        @pl.when((at < length) & (distance > 0))
        def _():
            k = me + distance * PAIR
            across(k, panel).wait_recv()

            @pl.when(has_down)
            def _():
                down(k, panel).start()

            @pl.when(panel < end_panel(at))
            def _():
                across(k, panel).start()

    def pass_low_end(distance):
        @pl.when((z == distance) & has_up)
        def _():
            for panel in range(panels - EXTRA, panels):
                k = 1 - x
                across(k, panel).wait_recv()
                if panel >= panels - TOP_EXTRA:
                    up(k, panel).start()
                else:

                    @pl.when(jnp.logical_not(is_near))
                    def _():
                        up(k, panel).start()

    def pass_high_end(distance):
        @pl.when((z + distance == last) & has_down)
        def _():
            for panel in range(panels - EXTRA, panels):
                k = last * PAIR + 1 - x
                across(k, panel).wait_recv()
                down(k, panel).start()

    def sends_done():
        @pl.loop(0, length)
        def sent(at):
            k = at * PAIR + x

            @pl.when(has_down & (at >= z))
            def _():
                wait_sent(1, k, 0, panels)

            short = is_near & (at >= last - NEAR) if far else False

            @pl.when(has_up & (at <= z) & jnp.logical_not(short))
            def _():
                wait_sent(0, k, 0, panels)

            @pl.when(has_up & (at <= z) & short)
            def _():
                wait_sent(0, k, 1, panels - 1)

            amount = end_panel(at) - first_panel(at)
            for size in sorted({panels, panels - 1, panels - EXTRA, panels - TOP_EXTRA}):

                @pl.when(amount == size)
                def _():
                    wait_sent(2, k, 0, size)

        @pl.when(has_up & is_near)
        def _():
            wait_sent(0, 1 - x, 0, TOP_EXTRA)

        @pl.when(has_up & jnp.logical_not(is_near))
        def _():
            wait_sent(0, 1 - x, 0, EXTRA)

        @pl.when(has_down)
        def _():
            wait_sent(1, last * PAIR + 1 - x, 0, EXTRA)

        if far:

            @pl.when(is_last)
            def _():
                for plane in range(NEAR):
                    far_down(plane).wait_send()

            @pl.when(is_near)
            def _():
                @pl.loop(1, cols // CORES)
                def peers(step):
                    who = (my_col + step * CORES) % cols
                    for plane in range(NEAR):
                        far_to(who, plane).wait_send()
                        far_move(who, plane, {"col": mate}, who, 1).wait_send()

                for plane in range(NEAR):
                    far_to(mate, plane).wait_send()

                far_result().wait_send()

    def split_in_two(value):
        high = value.astype(jnp.bfloat16)
        return high, (value - high.astype(jnp.float32)).astype(jnp.bfloat16)

    def right_of(at, panel):
        return gathered[pl.ds(at * PAIR, PAIR), panel].reshape(pair, block)

    def add_terms(distance):
        @pl.loop(0, 2)
        def each(way):
            at = z + (2 * way - 1) * distance

            @pl.when((at >= 0) & (at < length) & ((distance > 0) | ((distance == 0) & (way > 0))))
            def _():
                passed = ((at == 0) & has_up) | ((at == last) & has_down)

                first = first_panel(at)
                if far:
                    first = first + jnp.int32(is_near & (at >= last - NEAR) & (at < last))

                limit = panels - EXTRA * jnp.int32(passed)
                left_high = p_high[at]
                left_low = p_low[at]
                for begin in range(0, panels, GROUP):
                    for panel in range(begin, begin + GROUP):

                        @pl.when((panel >= first) & (panel < limit))
                        def _():
                            across(at * PAIR + 1 - x, panel).wait_recv()

                    right = jnp.concatenate(
                        [right_of(at, begin + panel) for panel in range(GROUP)], axis=1
                    )
                    high, low = split_in_two(right)
                    value = times(left_high, low) + times(left_low, high) + times(left_high, high)
                    here = slice(begin * block, (begin + GROUP) * block)
                    product[:, here] = product[:, here] + value

                if far:

                    @pl.when(is_last & (distance == last))
                    def _():
                        far_result().wait_recv()

    def forward_far(plane):
        far_to(mate, plane).wait_recv()

        @pl.loop(1, cols // CORES)
        def peers(step):
            far_to((my_col + step * CORES) % cols, plane).start()

        far_to(mate, plane).start()

    def mate_far(plane):
        @pl.loop(1, cols // CORES)
        def peers(step):
            who = (my_col + step * CORES) % cols
            far_move(who, plane, {"col": mate}, who, 1).wait_recv()
            far_move(who, plane, {"col": mate}, who, 1).start()

    def give_far():
        @pl.loop(0, cols // CORES)
        def mates(step):
            who = (mate + step * CORES) % cols
            for plane in range(NEAR):
                far_move(who, plane, {"col": mate}, who).wait_recv()

        value = None
        for plane in range(NEAR):
            at = last - NEAR + plane
            across(at * PAIR + 1 - x, 0).wait_recv()
            left_high, left_low = split_in_two(p_far[:, plane * pair : (plane + 1) * pair])
            high, low = split_in_two(right_of(at, 0))
            one = times(left_high, low) + times(left_low, high) + times(left_high, high)
            value = one if value is None else value + one
        far_part[...] = value
        far_result().start()

    product[...] = jnp.zeros_like(product)
    inner = jnp.int32((z > 0) & (z < last))

    @pl.loop(0, length + 2)
    def steps(distance):
        @pl.loop(0, panels)
        def lines(panel):
            pass_below(distance + 1, panel)
            ahead = distance * panels + panel + panels // 2
            pass_above(ahead // panels, ahead % panels)

        if far:

            @pl.when(is_near & (distance == 0))
            def _():
                for plane in range(NEAR):
                    forward_far(plane)

            @pl.when(is_near & (distance == 1))
            def _():
                for plane in range(NEAR):
                    mate_far(plane)

        pass_low_end(distance)
        pass_high_end(distance)
        if far:

            @pl.when(is_near & (distance == 1))
            def _():
                give_far()

        @pl.when(distance == length)
        def _():
            sends_done()

        add_terms(distance - 1 - inner)

    if far:

        @pl.when(is_last)
        def _():
            product[:, 0:block] = product[:, 0:block] + far_part[...]

    lane = 128
    squares = product[...] * product[...]
    squares = jnp.sum(squares.reshape(squares.shape[0] // 8, 8, width), axis=0)
    mine = squares[:, :lane]
    for panel in range(1, width // lane):
        mine = mine + squares[:, panel * lane : (panel + 1) * lane]
    spot = me * cols + my_col
    parts[spot, 0:1] = jnp.sum(mine, axis=0, keepdims=True)

    def part(slot, device):
        return pltpu.make_async_remote_copy(
            src_ref=parts.at[slot, pl.ds(0, 1)],
            dst_ref=parts.at[slot, pl.ds(0, 1)],
            send_sem=part_sem.at[0],
            recv_sem=part_sem.at[1],
            device_id={"blk": device // cols, "col": device % cols},
            device_id_type=MESH,
        )

    @pl.loop(0, total)
    def send_parts(device):
        @pl.when(device != spot)
        def _():
            part(spot, device).start()

    others = parts.at[pl.ds(0, total - 1), pl.ds(0, 1)]
    pltpu.make_async_copy(others, others, part_sem.at[0]).wait()
    pltpu.make_async_copy(others, others, part_sem.at[1]).wait()
    norm[...] = jnp.sum(parts[:, 0, :], axis=0, keepdims=True)


def finish(product_in, norm_in, product_out, norm_out, value, sem):
    store = pltpu.make_async_copy(product_in, product_out, sem.at[0])
    store.start()
    value[0] = jnp.sum(norm_in[...])
    send = pltpu.make_async_copy(value, norm_out, sem.at[1])
    send.start()
    store.wait()
    send.wait()


def solution(mesh):
    count = mesh.shape["blk"]
    cols = mesh.shape["col"]
    length = count // PAIR

    def per_device(
        density,
        occupied_p,
        hamil_dens,
        occupied_hp,
        window_sizes,
        row_window_sizes,
        slab_index,
        group_sizes,
    ):
        rows, inner = density.shape
        block, width = hamil_dens.shape
        hbm = pl.BlockSpec(memory_space=pltpu.HBM)
        vmem = pl.BlockSpec(memory_space=pltpu.VMEM)
        smem = pl.BlockSpec(memory_space=pltpu.SMEM)
        product, norm = pl.pallas_call(
            functools.partial(kernel, length, cols),
            out_shape=(
                pltpu.VMEM((rows, width), jnp.float32),
                pltpu.VMEM((1, 128), jnp.float32),
            ),
            in_specs=[hbm] * 8,
            out_specs=(vmem, vmem),
            scratch_shapes=[
                pltpu.VMEM((block, width), jnp.float32),
                pltpu.SMEM(occupied_p.shape, jnp.int32),
                pltpu.SMEM(occupied_hp.shape, jnp.int32),
                pltpu.SMEM(window_sizes.shape, jnp.int32),
                pltpu.SMEM(row_window_sizes.shape, jnp.int32),
                pltpu.SMEM(slab_index.shape, jnp.int32),
                pltpu.SMEM(group_sizes.shape, jnp.int32),
                pltpu.VMEM((count, width // block, block, block), jnp.float32),
                pltpu.VMEM((rows, inner), jnp.float32),
                pltpu.VMEM((length, rows, PAIR * block), jnp.bfloat16),
                pltpu.VMEM((length, rows, PAIR * block), jnp.bfloat16),
                pltpu.VMEM((rows, NEAR * PAIR * block), jnp.float32),
                pltpu.VMEM((rows, block), jnp.float32),
                pltpu.VMEM((count * cols, 8, 128), jnp.float32),
                pltpu.SemaphoreType.DMA((3, count)),
                pltpu.SemaphoreType.DMA((count, width // block)),
                pltpu.SemaphoreType.DMA((7 + width // block,)),
                pltpu.SemaphoreType.DMA((2,)),
                pltpu.SemaphoreType.DMA((2, cols, NEAR)),
                pltpu.SemaphoreType.DMA((cols, NEAR)),
                pltpu.SemaphoreType.DMA((2,)),
            ],
            compiler_params=pltpu.CompilerParams(
                collective_id=0, has_side_effects=True, vmem_limit_bytes=56 << 20
            ),
        )(
            *(
                pltpu.with_memory_space_constraint(value, pltpu.HBM)
                for value in (
                    density,
                    hamil_dens,
                    occupied_p,
                    occupied_hp,
                    window_sizes,
                    row_window_sizes,
                    slab_index,
                    group_sizes,
                )
            )
        )
        product, norm = pl.pallas_call(
            finish,
            out_shape=(
                jax.ShapeDtypeStruct((rows, width), jnp.float32),
                jax.ShapeDtypeStruct((1,), jnp.float32),
            ),
            in_specs=[vmem, vmem],
            out_specs=(hbm, hbm),
            scratch_shapes=[pltpu.SMEM((1,), jnp.float32), pltpu.SemaphoreType.DMA((2,))],
            compiler_params=pltpu.CompilerParams(vmem_limit_bytes=1 << 20),
        )(pltpu.with_memory_space_constraint(product, pltpu.VMEM), pltpu.with_memory_space_constraint(norm, pltpu.VMEM))
        return product, norm.reshape(())

    return jax.shard_map(
        per_device,
        mesh=mesh,
        in_specs=(
            P("blk", None),
            P("blk", None),
            P("blk", "col"),
            P("blk", "col"),
            P(),
            P(),
            P("col"),
            P(),
        ),
        out_specs=(P("blk", "col"), P()),
        check_vma=False,
    )
```

```python
import functools

import jax
import jax.numpy as jnp
from jax import lax
from jax.experimental import pallas as pl
from jax.experimental.pallas import tpu as pltpu
from jax.sharding import PartitionSpec as P

MESH = pl.DeviceIdType.MESH
PAIR = 2
EXTRA = 2
TOP_EXTRA = 1
NEAR = 2
CORES = 2
GROUP = 2
FAR_AFTER = 1


def kernel(
    length,
    cols,
    density,
    hamil_in,
    occ_p_in,
    occ_hp_in,
    window_in,
    row_window_in,
    slab_in,
    groups_in,
    product,
    norm,
    hamil,
    occ_p,
    occ_hp,
    window,
    row_window,
    slab,
    groups,
    gathered,
    p_in,
    p_high,
    p_low,
    p_far,
    far_part,
    parts,
    send_sem,
    recv_sem,
    load_sem,
    part_sem,
    far_send,
    far_recv,
    far_sem,
):
    count = length * PAIR
    total = count * cols
    block, width = hamil.shape
    row_blocks = product.shape[0] // block
    panels = width // block
    far = length >= NEAR + 2
    me = lax.axis_index("blk")
    my_col = lax.axis_index("col")
    z = me // PAIR
    x = me % PAIR
    partner = me + 1 - 2 * x
    last = length - 1
    has_up = z < last
    has_down = z > 0
    is_last = z == last
    is_near = z == last - 1

    loads = [
        pltpu.make_async_copy(source, target, load_sem.at[at])
        for at, (source, target) in enumerate(
            (
                (occ_hp_in, occ_hp),
                (window_in, window),
                (slab_in, slab),
                (groups_in, groups),
                (row_window_in, row_window),
                (occ_p_in, occ_p),
                (density, p_in),
            )
        )
    ]
    hamil_loads = [
        pltpu.make_async_copy(
            hamil_in.at[:, pl.ds(panel * block, block)],
            hamil.at[:, pl.ds(panel * block, block)],
            load_sem.at[len(loads) + panel],
        )
        for panel in range(panels)
    ]
    barrier = pltpu.get_barrier_semaphore()

    def greet(device):
        pl.semaphore_signal(barrier, inc=1, device_id=device, device_id_type=MESH)

    greet({"blk": partner})

    @pl.when(has_up)
    def _():
        greet({"blk": me + PAIR})

    @pl.when(has_down)
    def _():
        greet({"blk": me - PAIR})

    @pl.loop(1, cols)
    def greet_col(step):
        greet({"col": (my_col + step) % cols})

    for load in loads[:4] + hamil_loads + loads[4:]:
        load.start()

    for load in loads[:4]:
        load.wait()

    def move(where, k, panel, device):
        spot = gathered.at[k, panel]
        return pltpu.make_async_remote_copy(
            src_ref=spot,
            dst_ref=spot,
            send_sem=send_sem.at[where, k],
            recv_sem=recv_sem.at[k, panel],
            device_id={"blk": device},
            device_id_type=MESH,
        )

    def wait_sent(where, k, first, amount):
        spot = gathered.at[k, pl.ds(first, amount)]
        pltpu.make_async_copy(spot, spot, send_sem.at[where, k]).wait()

    def up(k, panel):
        return move(0, k, panel, me + PAIR)

    def down(k, panel):
        return move(1, k, panel, me - PAIR)

    def across(k, panel):
        return move(2, k, panel, partner)

    share = product.shape[0] // cols
    pair = PAIR * block

    mate = my_col + 1 - CORES * (my_col % CORES)

    def far_move(who, plane, device, sem, onward=0):
        spot = p_far.at[pl.ds(pl.multiple_of(who * share, share), share), pl.ds(plane * pair, pair)]
        return pltpu.make_async_remote_copy(
            src_ref=spot,
            dst_ref=spot,
            send_sem=far_send.at[onward, sem, plane],
            recv_sem=far_recv.at[who, plane],
            device_id=device,
            device_id_type=MESH,
        )

    def far_down(plane):
        return far_move(my_col, plane, {"blk": me - PAIR}, my_col)

    def far_to(peer, plane):
        return far_move(my_col, plane, {"col": peer}, peer)

    def far_result():
        return pltpu.make_async_remote_copy(
            src_ref=far_part,
            dst_ref=far_part,
            send_sem=far_sem.at[0],
            recv_sem=far_sem.at[1],
            device_id={"blk": me + PAIR},
            device_id_type=MESH,
        )

    row_at = lax.broadcasted_iota(jnp.int32, (block, block), 0)
    col_at = lax.broadcasted_iota(jnp.int32, (block, block), 1)

    def send_far():
        for load in loads[4:]:
            load.wait()
        first = my_col * share
        b = first // block
        share_row = lax.broadcasted_iota(jnp.int32, (share, block), 0) + first - b * block
        share_col = lax.broadcasted_iota(jnp.int32, (share, block), 1)
        rows = pl.ds(pl.multiple_of(first, share), share)
        live = share_row < row_window[me * row_blocks + b]
        for plane in range(NEAR):
            for other in range(PAIR):
                k = (last - NEAR + plane) * PAIR + other
                mask = jnp.where(
                    live & (share_col < window[k]), occ_p[b, k].astype(jnp.float32), 0.0
                )
                p_far[rows, pl.ds(plane * pair + other * block, block)] = (
                    p_in[rows, pl.ds(k * block, block)] * mask
                )
            far_down(plane).start()
        for plane in range(NEAR):
            for other in range(PAIR):
                k = (last - NEAR + plane) * PAIR + other
                gathered[k, 0] = jnp.zeros((block, block), jnp.float32)

    rows_live = row_at < window[me]
    for panel in range(panels):
        hamil_loads[panel].wait()
        size = groups[slab[panel]]
        occupied = occ_hp[0, panel].astype(jnp.float32)
        mask = jnp.where(rows_live & (col_at < size), occupied, 0.0)
        gathered[me, panel] = hamil[:, panel * block : (panel + 1) * block] * mask
        if panel == 0:
            ends = jnp.int32(z == 0) + jnp.int32(z == last)
            pl.semaphore_wait(barrier, PAIR - 1 + cols - 1 + 2 - ends)

        across(me, panel).start()
        if panel == 0 and far:

            @pl.when(has_up & jnp.logical_not(is_near))
            def _():
                up(me, panel).start()

        else:

            @pl.when(has_up)
            def _():
                up(me, panel).start()

        @pl.when(has_down)
        def _():
            down(me, panel).start()

        if panel == FAR_AFTER and far:
            pl.when(is_last)(send_far)

    def wait_loads():
        for load in loads[4:]:
            load.wait()

    if far:
        pl.when(jnp.logical_not(is_last))(wait_loads)
    else:
        wait_loads()

    @pl.loop(0, length)
    def split(at):
        for b in range(row_blocks):
            live = row_at < row_window[me * row_blocks + b]
            here = pl.ds(b * block, block)
            for other in range(PAIR):
                k = at * PAIR + other
                mask = jnp.where(
                    live & (col_at < window[k]), occ_p[b, k].astype(jnp.float32), 0.0
                )
                value = p_in[here, pl.ds(pl.multiple_of(k * block, block), block)] * mask
                high = value.astype(jnp.bfloat16)
                there = pl.ds(other * block, block)
                p_high[at, here, there] = high
                p_low[at, here, there] = (value - high.astype(jnp.float32)).astype(jnp.bfloat16)

    def times(a, b):
        return jnp.dot(a, b, preferred_element_type=jnp.float32)

    def first_panel(at):
        if not far:
            return 0
        return jnp.int32(is_last & (at >= last - NEAR) & (at < last))

    def end_panel(at):
        low = (at == 0) & (z > 0)
        high = (at == last) & (z < last)
        top = low & is_last
        return panels - EXTRA * jnp.int32(low | high) + (EXTRA - TOP_EXTRA) * jnp.int32(top)

    def pass_below(distance, panel):
        at = z - distance

        @pl.when((at >= 0) & (distance > 0) & (panel >= first_panel(at)))
        def _():
            k = me - distance * PAIR
            across(k, panel).wait_recv()
            skip = (panel == 0) & is_near & (at >= last - NEAR) if far else False

            @pl.when(has_up & jnp.logical_not(skip))
            def _():
                up(k, panel).start()

            @pl.when(panel < end_panel(at))
            def _():
                across(k, panel).start()

    def pass_above(distance, panel):
        at = z + distance

        @pl.when((at < length) & (distance > 0))
        def _():
            k = me + distance * PAIR
            across(k, panel).wait_recv()

            @pl.when(has_down)
            def _():
                down(k, panel).start()

            @pl.when(panel < end_panel(at))
            def _():
                across(k, panel).start()

    def pass_low_end(distance):
        @pl.when((z == distance) & has_up)
        def _():
            for panel in range(panels - EXTRA, panels):
                k = 1 - x
                across(k, panel).wait_recv()
                if panel >= panels - TOP_EXTRA:
                    up(k, panel).start()
                else:

                    @pl.when(jnp.logical_not(is_near))
                    def _():
                        up(k, panel).start()

    def pass_high_end(distance):
        @pl.when((z + distance == last) & has_down)
        def _():
            for panel in range(panels - EXTRA, panels):
                k = last * PAIR + 1 - x
                across(k, panel).wait_recv()
                down(k, panel).start()

    def sends_done():
        @pl.loop(0, length)
        def sent(at):
            k = at * PAIR + x

            @pl.when(has_down & (at >= z))
            def _():
                wait_sent(1, k, 0, panels)

            short = is_near & (at >= last - NEAR) if far else False

            @pl.when(has_up & (at <= z) & jnp.logical_not(short))
            def _():
                wait_sent(0, k, 0, panels)

            @pl.when(has_up & (at <= z) & short)
            def _():
                wait_sent(0, k, 1, panels - 1)

            amount = end_panel(at) - first_panel(at)
            for size in sorted({panels, panels - 1, panels - EXTRA, panels - TOP_EXTRA}):

                @pl.when(amount == size)
                def _():
                    wait_sent(2, k, 0, size)

        @pl.when(has_up & is_near)
        def _():
            wait_sent(0, 1 - x, 0, TOP_EXTRA)

        @pl.when(has_up & jnp.logical_not(is_near))
        def _():
            wait_sent(0, 1 - x, 0, EXTRA)

        @pl.when(has_down)
        def _():
            wait_sent(1, last * PAIR + 1 - x, 0, EXTRA)

        if far:

            @pl.when(is_last)
            def _():
                for plane in range(NEAR):
                    far_down(plane).wait_send()

            @pl.when(is_near)
            def _():
                @pl.loop(1, cols // CORES)
                def peers(step):
                    who = (my_col + step * CORES) % cols
                    for plane in range(NEAR):
                        far_to(who, plane).wait_send()
                        far_move(who, plane, {"col": mate}, who, 1).wait_send()

                for plane in range(NEAR):
                    far_to(mate, plane).wait_send()

                far_result().wait_send()

    def split_in_two(value):
        high = value.astype(jnp.bfloat16)
        return high, (value - high.astype(jnp.float32)).astype(jnp.bfloat16)

    def right_of(at, panel):
        return gathered[pl.ds(at * PAIR, PAIR), panel].reshape(pair, block)

    def add_terms(distance):
        @pl.loop(0, 2)
        def each(way):
            at = z + (2 * way - 1) * distance

            @pl.when((at >= 0) & (at < length) & ((distance > 0) | ((distance == 0) & (way > 0))))
            def _():
                passed = ((at == 0) & has_up) | ((at == last) & has_down)

                first = first_panel(at)
                if far:
                    first = first + jnp.int32(is_near & (at >= last - NEAR) & (at < last))

                limit = panels - EXTRA * jnp.int32(passed)
                left_high = p_high[at]
                left_low = p_low[at]
                for begin in range(0, panels, GROUP):
                    for panel in range(begin, begin + GROUP):

                        @pl.when((panel >= first) & (panel < limit))
                        def _():
                            across(at * PAIR + 1 - x, panel).wait_recv()

                    right = jnp.concatenate(
                        [right_of(at, begin + panel) for panel in range(GROUP)], axis=1
                    )
                    high, low = split_in_two(right)
                    value = times(left_high, low) + times(left_low, high) + times(left_high, high)
                    here = slice(begin * block, (begin + GROUP) * block)
                    product[:, here] = product[:, here] + value

    def forward_far(plane):
        far_to(mate, plane).wait_recv()

        @pl.loop(1, cols // CORES)
        def peers(step):
            far_to((my_col + step * CORES) % cols, plane).start()

        far_to(mate, plane).start()

    def mate_far(plane):
        @pl.loop(1, cols // CORES)
        def peers(step):
            who = (my_col + step * CORES) % cols
            far_move(who, plane, {"col": mate}, who, 1).wait_recv()
            far_move(who, plane, {"col": mate}, who, 1).start()

    def give_far():
        @pl.loop(0, cols // CORES)
        def mates(step):
            who = (mate + step * CORES) % cols
            for plane in range(NEAR):
                far_move(who, plane, {"col": mate}, who).wait_recv()

        value = None
        for plane in range(NEAR):
            at = last - NEAR + plane
            across(at * PAIR + 1 - x, 0).wait_recv()
            left_high, left_low = split_in_two(p_far[:, plane * pair : (plane + 1) * pair])
            high, low = split_in_two(right_of(at, 0))
            one = times(left_high, low) + times(left_low, high) + times(left_high, high)
            value = one if value is None else value + one
        far_part[...] = value
        far_result().start()

    product[...] = jnp.zeros_like(product)
    inner = jnp.int32((z > 0) & (z < last))

    @pl.loop(0, length + 1)
    def steps(distance):
        for panel in range(panels):
            pass_below(distance + 1, panel)
            ahead = panel + panels // 2
            pass_above(distance + ahead // panels, ahead % panels)

        if far:

            @pl.when(is_near & (distance == 0))
            def _():
                for plane in range(NEAR):
                    forward_far(plane)

            @pl.when(is_near & (distance == 1))
            def _():
                for plane in range(NEAR):
                    mate_far(plane)

        pass_low_end(distance)
        pass_high_end(distance)
        if far:

            @pl.when(is_near & (distance == 1))
            def _():
                give_far()

        @pl.when(distance == length)
        def _():
            sends_done()

        add_terms(distance - 1 - inner)

    def squares_of(panel):
        part_of = product[:, panel * block : (panel + 1) * block]
        return jnp.sum((part_of * part_of).reshape(part_of.shape[0] // 8, 8, block), axis=0)

    mine = squares_of(1)
    for panel in range(2, panels):
        mine = mine + squares_of(panel)
    if far:

        @pl.when(is_last)
        def _():
            far_result().wait_recv()
            product[:, 0:block] = product[:, 0:block] + far_part[...]

    mine = mine + squares_of(0)
    spot = me * cols + my_col
    parts[spot, 0:1] = jnp.sum(mine, axis=0, keepdims=True)

    def part(slot, device):
        return pltpu.make_async_remote_copy(
            src_ref=parts.at[slot, pl.ds(0, 1)],
            dst_ref=parts.at[slot, pl.ds(0, 1)],
            send_sem=part_sem.at[0],
            recv_sem=part_sem.at[1],
            device_id={"blk": device // cols, "col": device % cols},
            device_id_type=MESH,
        )

    @pl.loop(0, total)
    def send_parts(device):
        @pl.when(device != spot)
        def _():
            part(spot, device).start()

    others = parts.at[pl.ds(0, total - 1), pl.ds(0, 1)]
    pltpu.make_async_copy(others, others, part_sem.at[0]).wait()
    pltpu.make_async_copy(others, others, part_sem.at[1]).wait()
    norm[...] = jnp.sum(parts[:, 0, :], axis=0, keepdims=True)


def finish(product_in, norm_in, product_out, norm_out, value, sem):
    store = pltpu.make_async_copy(product_in, product_out, sem.at[0])
    store.start()
    value[0] = jnp.sum(norm_in[...])
    send = pltpu.make_async_copy(value, norm_out, sem.at[1])
    send.start()
    store.wait()
    send.wait()


def solution(mesh):
    count = mesh.shape["blk"]
    cols = mesh.shape["col"]
    length = count // PAIR

    def per_device(
        density,
        occupied_p,
        hamil_dens,
        occupied_hp,
        window_sizes,
        row_window_sizes,
        slab_index,
        group_sizes,
    ):
        rows, inner = density.shape
        block, width = hamil_dens.shape
        hbm = pl.BlockSpec(memory_space=pltpu.HBM)
        vmem = pl.BlockSpec(memory_space=pltpu.VMEM)
        smem = pl.BlockSpec(memory_space=pltpu.SMEM)
        product, norm = pl.pallas_call(
            functools.partial(kernel, length, cols),
            out_shape=(
                pltpu.VMEM((rows, width), jnp.float32),
                pltpu.VMEM((1, 128), jnp.float32),
            ),
            in_specs=[hbm] * 8,
            out_specs=(vmem, vmem),
            scratch_shapes=[
                pltpu.VMEM((block, width), jnp.float32),
                pltpu.SMEM(occupied_p.shape, jnp.int32),
                pltpu.SMEM(occupied_hp.shape, jnp.int32),
                pltpu.SMEM(window_sizes.shape, jnp.int32),
                pltpu.SMEM(row_window_sizes.shape, jnp.int32),
                pltpu.SMEM(slab_index.shape, jnp.int32),
                pltpu.SMEM(group_sizes.shape, jnp.int32),
                pltpu.VMEM((count, width // block, block, block), jnp.float32),
                pltpu.VMEM((rows, inner), jnp.float32),
                pltpu.VMEM((length, rows, PAIR * block), jnp.bfloat16),
                pltpu.VMEM((length, rows, PAIR * block), jnp.bfloat16),
                pltpu.VMEM((rows, NEAR * PAIR * block), jnp.float32),
                pltpu.VMEM((rows, block), jnp.float32),
                pltpu.VMEM((count * cols, 8, 128), jnp.float32),
                pltpu.SemaphoreType.DMA((3, count)),
                pltpu.SemaphoreType.DMA((count, width // block)),
                pltpu.SemaphoreType.DMA((7 + width // block,)),
                pltpu.SemaphoreType.DMA((2,)),
                pltpu.SemaphoreType.DMA((2, cols, NEAR)),
                pltpu.SemaphoreType.DMA((cols, NEAR)),
                pltpu.SemaphoreType.DMA((2,)),
            ],
            compiler_params=pltpu.CompilerParams(
                collective_id=0, has_side_effects=True, vmem_limit_bytes=56 << 20
            ),
        )(
            *(
                pltpu.with_memory_space_constraint(value, pltpu.HBM)
                for value in (
                    density,
                    hamil_dens,
                    occupied_p,
                    occupied_hp,
                    window_sizes,
                    row_window_sizes,
                    slab_index,
                    group_sizes,
                )
            )
        )
        product, norm = pl.pallas_call(
            finish,
            out_shape=(
                jax.ShapeDtypeStruct((rows, width), jnp.float32),
                jax.ShapeDtypeStruct((1,), jnp.float32),
            ),
            in_specs=[vmem, vmem],
            out_specs=(hbm, hbm),
            scratch_shapes=[pltpu.SMEM((1,), jnp.float32), pltpu.SemaphoreType.DMA((2,))],
            compiler_params=pltpu.CompilerParams(vmem_limit_bytes=1 << 20),
        )(pltpu.with_memory_space_constraint(product, pltpu.VMEM), pltpu.with_memory_space_constraint(norm, pltpu.VMEM))
        return product, norm.reshape(())

    return jax.shard_map(
        per_device,
        mesh=mesh,
        in_specs=(
            P("blk", None),
            P("blk", None),
            P("blk", "col"),
            P("blk", "col"),
            P(),
            P(),
            P("col"),
            P(),
        ),
        out_specs=(P("blk", "col"), P()),
        check_vma=False,
    )
```

```python
import functools

import jax
import jax.numpy as jnp
from jax import lax
from jax.experimental import pallas as pl
from jax.experimental.pallas import tpu as pltpu
from jax.sharding import PartitionSpec as P

MESH = pl.DeviceIdType.MESH
PAIR = 2
EXTRA = 2
TOP_EXTRA = 1
NEAR = 2
CORES = 2
GROUP = 2
FAR_AFTER = 0


def kernel(
    length,
    cols,
    density,
    hamil_in,
    occ_p_in,
    occ_hp_in,
    window_in,
    row_window_in,
    slab_in,
    groups_in,
    product,
    norm,
    hamil,
    occ_p,
    occ_hp,
    window,
    row_window,
    slab,
    groups,
    gathered,
    p_in,
    p_high,
    p_low,
    p_far,
    far_part,
    parts,
    send_sem,
    recv_sem,
    load_sem,
    part_sem,
    far_send,
    far_recv,
    far_sem,
):
    count = length * PAIR
    total = count * cols
    block, width = hamil.shape
    row_blocks = product.shape[0] // block
    panels = width // block
    far = length >= NEAR + 2
    me = lax.axis_index("blk")
    my_col = lax.axis_index("col")
    z = me // PAIR
    x = me % PAIR
    partner = me + 1 - 2 * x
    last = length - 1
    has_up = z < last
    has_down = z > 0
    is_last = z == last
    is_near = z == last - 1

    loads = [
        pltpu.make_async_copy(source, target, load_sem.at[at])
        for at, (source, target) in enumerate(
            (
                (occ_hp_in, occ_hp),
                (window_in, window),
                (slab_in, slab),
                (groups_in, groups),
                (row_window_in, row_window),
                (occ_p_in, occ_p),
                (density, p_in),
            )
        )
    ]
    hamil_loads = [
        pltpu.make_async_copy(
            hamil_in.at[:, pl.ds(panel * block, block)],
            hamil.at[:, pl.ds(panel * block, block)],
            load_sem.at[len(loads) + panel],
        )
        for panel in range(panels)
    ]
    barrier = pltpu.get_barrier_semaphore()

    def greet(device):
        pl.semaphore_signal(barrier, inc=1, device_id=device, device_id_type=MESH)

    greet({"blk": partner})

    @pl.when(has_up)
    def _():
        greet({"blk": me + PAIR})

    @pl.when(has_down)
    def _():
        greet({"blk": me - PAIR})

    @pl.loop(1, cols)
    def greet_col(step):
        greet({"col": (my_col + step) % cols})

    for load in loads[:4] + hamil_loads + loads[4:]:
        load.start()

    for load in loads[:4]:
        load.wait()

    def move(where, k, panel, device):
        spot = gathered.at[k, panel]
        return pltpu.make_async_remote_copy(
            src_ref=spot,
            dst_ref=spot,
            send_sem=send_sem.at[where, k],
            recv_sem=recv_sem.at[k, panel],
            device_id={"blk": device},
            device_id_type=MESH,
        )

    def wait_sent(where, k, first, amount):
        spot = gathered.at[k, pl.ds(first, amount)]
        pltpu.make_async_copy(spot, spot, send_sem.at[where, k]).wait()

    def up(k, panel):
        return move(0, k, panel, me + PAIR)

    def down(k, panel):
        return move(1, k, panel, me - PAIR)

    def across(k, panel):
        return move(2, k, panel, partner)

    share = product.shape[0] // cols
    pair = PAIR * block

    mate = my_col + 1 - CORES * (my_col % CORES)

    def far_move(who, plane, device, sem, onward=0):
        spot = p_far.at[pl.ds(pl.multiple_of(who * share, share), share), pl.ds(plane * pair, pair)]
        return pltpu.make_async_remote_copy(
            src_ref=spot,
            dst_ref=spot,
            send_sem=far_send.at[onward, sem, plane],
            recv_sem=far_recv.at[who, plane],
            device_id=device,
            device_id_type=MESH,
        )

    def far_down(plane):
        return far_move(my_col, plane, {"blk": me - PAIR}, my_col)

    def far_to(peer, plane):
        return far_move(my_col, plane, {"col": peer}, peer)

    def far_result():
        return pltpu.make_async_remote_copy(
            src_ref=far_part,
            dst_ref=far_part,
            send_sem=far_sem.at[0],
            recv_sem=far_sem.at[1],
            device_id={"blk": me + PAIR},
            device_id_type=MESH,
        )

    row_at = lax.broadcasted_iota(jnp.int32, (block, block), 0)
    col_at = lax.broadcasted_iota(jnp.int32, (block, block), 1)

    def send_far():
        for load in loads[4:]:
            load.wait()
        first = my_col * share
        b = first // block
        share_row = lax.broadcasted_iota(jnp.int32, (share, block), 0) + first - b * block
        share_col = lax.broadcasted_iota(jnp.int32, (share, block), 1)
        rows = pl.ds(pl.multiple_of(first, share), share)
        live = share_row < row_window[me * row_blocks + b]
        for plane in range(NEAR):
            for other in range(PAIR):
                k = (last - NEAR + plane) * PAIR + other
                mask = jnp.where(
                    live & (share_col < window[k]), occ_p[b, k].astype(jnp.float32), 0.0
                )
                p_far[rows, pl.ds(plane * pair + other * block, block)] = (
                    p_in[rows, pl.ds(k * block, block)] * mask
                )
            far_down(plane).start()
        for plane in range(NEAR):
            for other in range(PAIR):
                k = (last - NEAR + plane) * PAIR + other
                gathered[k, 0] = jnp.zeros((block, block), jnp.float32)

    rows_live = row_at < window[me]
    for panel in range(panels):
        hamil_loads[panel].wait()
        size = groups[slab[panel]]
        occupied = occ_hp[0, panel].astype(jnp.float32)
        mask = jnp.where(rows_live & (col_at < size), occupied, 0.0)
        gathered[me, panel] = hamil[:, panel * block : (panel + 1) * block] * mask
        if panel == 0:
            ends = jnp.int32(z == 0) + jnp.int32(z == last)
            pl.semaphore_wait(barrier, PAIR - 1 + cols - 1 + 2 - ends)

        across(me, panel).start()
        if panel == 0 and far:

            @pl.when(has_up & jnp.logical_not(is_near))
            def _():
                up(me, panel).start()

        else:

            @pl.when(has_up)
            def _():
                up(me, panel).start()

        @pl.when(has_down)
        def _():
            down(me, panel).start()

        if panel == FAR_AFTER and far:
            pl.when(is_last)(send_far)

    def wait_loads():
        for load in loads[4:]:
            load.wait()

    if far:
        pl.when(jnp.logical_not(is_last))(wait_loads)
    else:
        wait_loads()

    @pl.loop(0, length)
    def split(at):
        for b in range(row_blocks):
            live = row_at < row_window[me * row_blocks + b]
            here = pl.ds(b * block, block)
            for other in range(PAIR):
                k = at * PAIR + other
                mask = jnp.where(
                    live & (col_at < window[k]), occ_p[b, k].astype(jnp.float32), 0.0
                )
                value = p_in[here, pl.ds(pl.multiple_of(k * block, block), block)] * mask
                high = value.astype(jnp.bfloat16)
                there = pl.ds(other * block, block)
                p_high[at, here, there] = high
                p_low[at, here, there] = (value - high.astype(jnp.float32)).astype(jnp.bfloat16)

    def times(a, b):
        return jnp.dot(a, b, preferred_element_type=jnp.float32)

    def first_panel(at):
        if not far:
            return 0
        return jnp.int32(is_last & (at >= last - NEAR) & (at < last))

    def end_panel(at):
        low = (at == 0) & (z > 0)
        high = (at == last) & (z < last)
        top = low & is_last
        return panels - EXTRA * jnp.int32(low | high) + (EXTRA - TOP_EXTRA) * jnp.int32(top)

    def pass_below(distance, panel):
        at = z - distance

        @pl.when((at >= 0) & (distance > 0) & (panel >= first_panel(at)))
        def _():
            k = me - distance * PAIR
            across(k, panel).wait_recv()
            skip = (panel == 0) & is_near & (at >= last - NEAR) if far else False

            @pl.when(has_up & jnp.logical_not(skip))
            def _():
                up(k, panel).start()

            @pl.when(panel < end_panel(at))
            def _():
                across(k, panel).start()

    def pass_above(distance, panel):
        at = z + distance

        @pl.when((at < length) & (distance > 0))
        def _():
            k = me + distance * PAIR
            across(k, panel).wait_recv()

            @pl.when(has_down)
            def _():
                down(k, panel).start()

            @pl.when(panel < end_panel(at))
            def _():
                across(k, panel).start()

    def pass_low_end(distance):
        @pl.when((z == distance) & has_up)
        def _():
            for panel in range(panels - EXTRA, panels):
                k = 1 - x
                across(k, panel).wait_recv()
                if panel >= panels - TOP_EXTRA:
                    up(k, panel).start()
                else:

                    @pl.when(jnp.logical_not(is_near))
                    def _():
                        up(k, panel).start()

    def pass_high_end(distance):
        @pl.when((z + distance == last) & has_down)
        def _():
            for panel in range(panels - EXTRA, panels):
                k = last * PAIR + 1 - x
                across(k, panel).wait_recv()
                down(k, panel).start()

    def sends_done():
        @pl.loop(0, length)
        def sent(at):
            k = at * PAIR + x

            @pl.when(has_down & (at >= z))
            def _():
                wait_sent(1, k, 0, panels)

            short = is_near & (at >= last - NEAR) if far else False

            @pl.when(has_up & (at <= z) & jnp.logical_not(short))
            def _():
                wait_sent(0, k, 0, panels)

            @pl.when(has_up & (at <= z) & short)
            def _():
                wait_sent(0, k, 1, panels - 1)

            amount = end_panel(at) - first_panel(at)
            for size in sorted({panels, panels - 1, panels - EXTRA, panels - TOP_EXTRA}):

                @pl.when(amount == size)
                def _():
                    wait_sent(2, k, 0, size)

        @pl.when(has_up & is_near)
        def _():
            wait_sent(0, 1 - x, 0, TOP_EXTRA)

        @pl.when(has_up & jnp.logical_not(is_near))
        def _():
            wait_sent(0, 1 - x, 0, EXTRA)

        @pl.when(has_down)
        def _():
            wait_sent(1, last * PAIR + 1 - x, 0, EXTRA)

        if far:

            @pl.when(is_last)
            def _():
                for plane in range(NEAR):
                    far_down(plane).wait_send()

            @pl.when(is_near)
            def _():
                @pl.loop(1, cols // CORES)
                def peers(step):
                    who = (my_col + step * CORES) % cols
                    for plane in range(NEAR):
                        far_to(who, plane).wait_send()
                        far_move(who, plane, {"col": mate}, who, 1).wait_send()

                for plane in range(NEAR):
                    far_to(mate, plane).wait_send()

                far_result().wait_send()

    def split_in_two(value):
        high = value.astype(jnp.bfloat16)
        return high, (value - high.astype(jnp.float32)).astype(jnp.bfloat16)

    def right_of(at, panel):
        return gathered[pl.ds(at * PAIR, PAIR), panel].reshape(pair, block)

    def add_terms(distance):
        @pl.loop(0, 2)
        def each(way):
            at = z + (2 * way - 1) * distance

            @pl.when((at >= 0) & (at < length) & ((distance > 0) | ((distance == 0) & (way > 0))))
            def _():
                passed = ((at == 0) & has_up) | ((at == last) & has_down)

                first = first_panel(at)
                if far:
                    first = first + jnp.int32(is_near & (at >= last - NEAR) & (at < last))

                limit = panels - EXTRA * jnp.int32(passed)
                left_high = p_high[at]
                left_low = p_low[at]
                for begin in range(0, panels, GROUP):
                    for panel in range(begin, begin + GROUP):

                        @pl.when((panel >= first) & (panel < limit))
                        def _():
                            across(at * PAIR + 1 - x, panel).wait_recv()

                    right = jnp.concatenate(
                        [right_of(at, begin + panel) for panel in range(GROUP)], axis=1
                    )
                    high, low = split_in_two(right)
                    value = times(left_high, low) + times(left_low, high) + times(left_high, high)
                    here = slice(begin * block, (begin + GROUP) * block)
                    product[:, here] = product[:, here] + value

    def forward_far(plane):
        far_to(mate, plane).wait_recv()

        @pl.loop(1, cols // CORES)
        def peers(step):
            far_to((my_col + step * CORES) % cols, plane).start()

        far_to(mate, plane).start()

    def mate_far(plane):
        @pl.loop(1, cols // CORES)
        def peers(step):
            who = (my_col + step * CORES) % cols
            far_move(who, plane, {"col": mate}, who, 1).wait_recv()
            far_move(who, plane, {"col": mate}, who, 1).start()

    def give_far():
        @pl.loop(0, cols // CORES)
        def mates(step):
            who = (mate + step * CORES) % cols
            for plane in range(NEAR):
                far_move(who, plane, {"col": mate}, who).wait_recv()

        value = None
        for plane in range(NEAR):
            at = last - NEAR + plane
            across(at * PAIR + 1 - x, 0).wait_recv()
            left_high, left_low = split_in_two(p_far[:, plane * pair : (plane + 1) * pair])
            high, low = split_in_two(right_of(at, 0))
            one = times(left_high, low) + times(left_low, high) + times(left_high, high)
            value = one if value is None else value + one
        far_part[...] = value
        far_result().start()

    product[...] = jnp.zeros_like(product)
    inner = 0

    @pl.loop(0, length + 1)
    def steps(distance):
        for panel in range(panels):
            pass_below(distance + 1, panel)
            if far and panel >= panels - NEAR:

                @pl.when(is_near & (distance == 0))
                def _():
                    forward_far(panel - panels + NEAR)

            ahead = panel + panels // 2
            pass_above(distance + ahead // panels, ahead % panels)

        if far:

            @pl.when(is_near & (distance == 1))
            def _():
                for plane in range(NEAR):
                    mate_far(plane)

        pass_low_end(distance)
        pass_high_end(distance)
        if far:

            @pl.when(is_near & (distance == 1))
            def _():
                give_far()

        @pl.when(distance == length)
        def _():
            sends_done()

        add_terms(distance - 1 - inner)

    def squares_of(panel):
        part_of = product[:, panel * block : (panel + 1) * block]
        return jnp.sum((part_of * part_of).reshape(part_of.shape[0] // 8, 8, block), axis=0)

    mine = squares_of(1)
    for panel in range(2, panels):
        mine = mine + squares_of(panel)
    if far:

        @pl.when(is_last)
        def _():
            far_result().wait_recv()
            product[:, 0:block] = product[:, 0:block] + far_part[...]

    mine = mine + squares_of(0)
    spot = me * cols + my_col
    parts[spot, 0:1] = jnp.sum(mine, axis=0, keepdims=True)

    def part(slot, device):
        return pltpu.make_async_remote_copy(
            src_ref=parts.at[slot, pl.ds(0, 1)],
            dst_ref=parts.at[slot, pl.ds(0, 1)],
            send_sem=part_sem.at[0],
            recv_sem=part_sem.at[1],
            device_id={"blk": device // cols, "col": device % cols},
            device_id_type=MESH,
        )

    @pl.loop(0, total)
    def send_parts(device):
        @pl.when(device != spot)
        def _():
            part(spot, device).start()

    others = parts.at[pl.ds(0, total - 1), pl.ds(0, 1)]
    pltpu.make_async_copy(others, others, part_sem.at[0]).wait()
    pltpu.make_async_copy(others, others, part_sem.at[1]).wait()
    norm[...] = jnp.sum(parts[:, 0, :], axis=0, keepdims=True)


def finish(product_in, norm_in, product_out, norm_out, value, sem):
    store = pltpu.make_async_copy(product_in, product_out, sem.at[0])
    store.start()
    value[0] = jnp.sum(norm_in[...])
    send = pltpu.make_async_copy(value, norm_out, sem.at[1])
    send.start()
    store.wait()
    send.wait()


def solution(mesh):
    count = mesh.shape["blk"]
    cols = mesh.shape["col"]
    length = count // PAIR

    def per_device(
        density,
        occupied_p,
        hamil_dens,
        occupied_hp,
        window_sizes,
        row_window_sizes,
        slab_index,
        group_sizes,
    ):
        rows, inner = density.shape
        block, width = hamil_dens.shape
        hbm = pl.BlockSpec(memory_space=pltpu.HBM)
        vmem = pl.BlockSpec(memory_space=pltpu.VMEM)
        smem = pl.BlockSpec(memory_space=pltpu.SMEM)
        product, norm = pl.pallas_call(
            functools.partial(kernel, length, cols),
            out_shape=(
                pltpu.VMEM((rows, width), jnp.float32),
                pltpu.VMEM((1, 128), jnp.float32),
            ),
            in_specs=[hbm] * 8,
            out_specs=(vmem, vmem),
            scratch_shapes=[
                pltpu.VMEM((block, width), jnp.float32),
                pltpu.SMEM(occupied_p.shape, jnp.int32),
                pltpu.SMEM(occupied_hp.shape, jnp.int32),
                pltpu.SMEM(window_sizes.shape, jnp.int32),
                pltpu.SMEM(row_window_sizes.shape, jnp.int32),
                pltpu.SMEM(slab_index.shape, jnp.int32),
                pltpu.SMEM(group_sizes.shape, jnp.int32),
                pltpu.VMEM((count, width // block, block, block), jnp.float32),
                pltpu.VMEM((rows, inner), jnp.float32),
                pltpu.VMEM((length, rows, PAIR * block), jnp.bfloat16),
                pltpu.VMEM((length, rows, PAIR * block), jnp.bfloat16),
                pltpu.VMEM((rows, NEAR * PAIR * block), jnp.float32),
                pltpu.VMEM((rows, block), jnp.float32),
                pltpu.VMEM((count * cols, 8, 128), jnp.float32),
                pltpu.SemaphoreType.DMA((3, count)),
                pltpu.SemaphoreType.DMA((count, width // block)),
                pltpu.SemaphoreType.DMA((7 + width // block,)),
                pltpu.SemaphoreType.DMA((2,)),
                pltpu.SemaphoreType.DMA((2, cols, NEAR)),
                pltpu.SemaphoreType.DMA((cols, NEAR)),
                pltpu.SemaphoreType.DMA((2,)),
            ],
            compiler_params=pltpu.CompilerParams(
                collective_id=0, has_side_effects=True, vmem_limit_bytes=56 << 20
            ),
        )(
            *(
                pltpu.with_memory_space_constraint(value, pltpu.HBM)
                for value in (
                    density,
                    hamil_dens,
                    occupied_p,
                    occupied_hp,
                    window_sizes,
                    row_window_sizes,
                    slab_index,
                    group_sizes,
                )
            )
        )
        product, norm = pl.pallas_call(
            finish,
            out_shape=(
                jax.ShapeDtypeStruct((rows, width), jnp.float32),
                jax.ShapeDtypeStruct((1,), jnp.float32),
            ),
            in_specs=[vmem, vmem],
            out_specs=(hbm, hbm),
            scratch_shapes=[pltpu.SMEM((1,), jnp.float32), pltpu.SemaphoreType.DMA((2,))],
            compiler_params=pltpu.CompilerParams(vmem_limit_bytes=1 << 20),
        )(pltpu.with_memory_space_constraint(product, pltpu.VMEM), pltpu.with_memory_space_constraint(norm, pltpu.VMEM))
        return product, norm.reshape(())

    return jax.shard_map(
        per_device,
        mesh=mesh,
        in_specs=(
            P("blk", None),
            P("blk", None),
            P("blk", "col"),
            P("blk", "col"),
            P(),
            P(),
            P("col"),
            P(),
        ),
        out_specs=(P("blk", "col"), P()),
        check_vma=False,
    )
```

```python
import functools

import jax
import jax.numpy as jnp
from jax import lax
from jax.experimental import pallas as pl
from jax.experimental.pallas import tpu as pltpu
from jax.sharding import PartitionSpec as P

MESH = pl.DeviceIdType.MESH
PAIR = 2
EXTRA = 2
TOP_EXTRA = 1
NEAR = 2
CORES = 2
GROUP = 2
FAR_AFTER = 0


def kernel(
    length,
    cols,
    density,
    hamil_in,
    occ_p_in,
    occ_hp_in,
    window_in,
    row_window_in,
    slab_in,
    groups_in,
    product,
    norm,
    hamil,
    occ_p,
    occ_hp,
    window,
    row_window,
    slab,
    groups,
    gathered,
    p_in,
    p_high,
    p_low,
    p_far,
    far_part,
    parts,
    send_sem,
    recv_sem,
    load_sem,
    part_sem,
    far_send,
    far_recv,
    far_sem,
):
    count = length * PAIR
    total = count * cols
    block, width = hamil.shape
    row_blocks = product.shape[0] // block
    panels = width // block
    far = length >= NEAR + 2
    me = lax.axis_index("blk")
    my_col = lax.axis_index("col")
    z = me // PAIR
    x = me % PAIR
    partner = me + 1 - 2 * x
    last = length - 1
    has_up = z < last
    has_down = z > 0
    is_last = z == last
    is_near = z == last - 1

    loads = [
        pltpu.make_async_copy(source, target, load_sem.at[at])
        for at, (source, target) in enumerate(
            (
                (occ_hp_in, occ_hp),
                (window_in, window),
                (slab_in, slab),
                (groups_in, groups),
                (row_window_in, row_window),
                (occ_p_in, occ_p),
                (density, p_in),
            )
        )
    ]
    hamil_loads = [
        pltpu.make_async_copy(
            hamil_in.at[:, pl.ds(panel * block, block)],
            hamil.at[:, pl.ds(panel * block, block)],
            load_sem.at[len(loads) + panel],
        )
        for panel in range(panels)
    ]
    barrier = pltpu.get_barrier_semaphore()

    def greet(device):
        pl.semaphore_signal(barrier, inc=1, device_id=device, device_id_type=MESH)

    greet({"blk": partner})

    @pl.when(has_up)
    def _():
        greet({"blk": me + PAIR})

    @pl.when(has_down)
    def _():
        greet({"blk": me - PAIR})

    @pl.loop(1, cols)
    def greet_col(step):
        greet({"col": (my_col + step) % cols})

    for load in loads[:4] + hamil_loads + loads[4:]:
        load.start()

    for load in loads[:4]:
        load.wait()

    def move(where, k, panel, device):
        spot = gathered.at[k, panel]
        return pltpu.make_async_remote_copy(
            src_ref=spot,
            dst_ref=spot,
            send_sem=send_sem.at[where, k],
            recv_sem=recv_sem.at[k, panel],
            device_id={"blk": device},
            device_id_type=MESH,
        )

    def wait_sent(where, k, first, amount):
        spot = gathered.at[k, pl.ds(first, amount)]
        pltpu.make_async_copy(spot, spot, send_sem.at[where, k]).wait()

    def up(k, panel):
        return move(0, k, panel, me + PAIR)

    def down(k, panel):
        return move(1, k, panel, me - PAIR)

    def across(k, panel):
        return move(2, k, panel, partner)

    share = product.shape[0] // cols
    pair = PAIR * block

    mate = my_col + 1 - CORES * (my_col % CORES)

    def far_move(who, plane, device, sem, onward=0):
        spot = p_far.at[pl.ds(pl.multiple_of(who * share, share), share), pl.ds(plane * pair, pair)]
        return pltpu.make_async_remote_copy(
            src_ref=spot,
            dst_ref=spot,
            send_sem=far_send.at[onward, sem, plane],
            recv_sem=far_recv.at[who, plane],
            device_id=device,
            device_id_type=MESH,
        )

    def far_down(plane):
        return far_move(my_col, plane, {"blk": me - PAIR}, my_col)

    def far_to(peer, plane):
        return far_move(my_col, plane, {"col": peer}, peer)

    def far_result():
        return pltpu.make_async_remote_copy(
            src_ref=far_part,
            dst_ref=far_part,
            send_sem=far_sem.at[0],
            recv_sem=far_sem.at[1],
            device_id={"blk": me + PAIR},
            device_id_type=MESH,
        )

    row_at = lax.broadcasted_iota(jnp.int32, (block, block), 0)
    col_at = lax.broadcasted_iota(jnp.int32, (block, block), 1)

    def send_far():
        for load in loads[4:]:
            load.wait()
        first = my_col * share
        b = first // block
        share_row = lax.broadcasted_iota(jnp.int32, (share, block), 0) + first - b * block
        share_col = lax.broadcasted_iota(jnp.int32, (share, block), 1)
        rows = pl.ds(pl.multiple_of(first, share), share)
        live = share_row < row_window[me * row_blocks + b]
        for plane in range(NEAR):
            for other in range(PAIR):
                k = (last - NEAR + plane) * PAIR + other
                mask = jnp.where(
                    live & (share_col < window[k]), occ_p[b, k].astype(jnp.float32), 0.0
                )
                p_far[rows, pl.ds(plane * pair + other * block, block)] = (
                    p_in[rows, pl.ds(k * block, block)] * mask
                )
            far_down(plane).start()
        for plane in range(NEAR):
            for other in range(PAIR):
                k = (last - NEAR + plane) * PAIR + other
                gathered[k, 0] = jnp.zeros((block, block), jnp.float32)

    rows_live = row_at < window[me]
    for panel in range(panels):
        hamil_loads[panel].wait()
        size = groups[slab[panel]]
        occupied = occ_hp[0, panel].astype(jnp.float32)
        mask = jnp.where(rows_live & (col_at < size), occupied, 0.0)
        gathered[me, panel] = hamil[:, panel * block : (panel + 1) * block] * mask
        if panel == 0:
            ends = jnp.int32(z == 0) + jnp.int32(z == last)
            pl.semaphore_wait(barrier, PAIR - 1 + cols - 1 + 2 - ends)

        across(me, panel).start()
        if panel == 0 and far:

            @pl.when(has_up & jnp.logical_not(is_near))
            def _():
                up(me, panel).start()

        else:

            @pl.when(has_up)
            def _():
                up(me, panel).start()

        @pl.when(has_down)
        def _():
            down(me, panel).start()

        if panel == FAR_AFTER and far:
            pl.when(is_last)(send_far)

    def wait_loads():
        for load in loads[4:]:
            load.wait()

    if far:
        pl.when(jnp.logical_not(is_last))(wait_loads)
    else:
        wait_loads()

    @pl.loop(0, length)
    def split(at):
        for b in range(row_blocks):
            live = row_at < row_window[me * row_blocks + b]
            here = pl.ds(b * block, block)
            for other in range(PAIR):
                k = at * PAIR + other
                mask = jnp.where(
                    live & (col_at < window[k]), occ_p[b, k].astype(jnp.float32), 0.0
                )
                value = p_in[here, pl.ds(pl.multiple_of(k * block, block), block)] * mask
                high = value.astype(jnp.bfloat16)
                there = pl.ds(other * block, block)
                p_high[at, here, there] = high
                p_low[at, here, there] = (value - high.astype(jnp.float32)).astype(jnp.bfloat16)

    def times(a, b):
        return jnp.dot(a, b, preferred_element_type=jnp.float32)

    def first_panel(at):
        if not far:
            return 0
        return jnp.int32(is_last & (at >= last - NEAR) & (at < last))

    def end_panel(at):
        low = (at == 0) & (z > 0)
        high = (at == last) & (z < last)
        top = low & is_last
        return panels - EXTRA * jnp.int32(low | high) + (EXTRA - TOP_EXTRA) * jnp.int32(top)

    def pass_below(distance, panel):
        at = z - distance

        @pl.when((at >= 0) & (distance > 0) & (panel >= first_panel(at)))
        def _():
            k = me - distance * PAIR
            across(k, panel).wait_recv()
            skip = (panel == 0) & is_near & (at >= last - NEAR) if far else False

            @pl.when(has_up & jnp.logical_not(skip))
            def _():
                up(k, panel).start()

            @pl.when(panel < end_panel(at))
            def _():
                across(k, panel).start()

    def pass_above(distance, panel):
        at = z + distance

        @pl.when((at < length) & (distance > 0))
        def _():
            k = me + distance * PAIR
            across(k, panel).wait_recv()

            @pl.when(has_down)
            def _():
                down(k, panel).start()

            @pl.when(panel < end_panel(at))
            def _():
                across(k, panel).start()

    def pass_low_end(distance):
        @pl.when((z == distance) & has_up)
        def _():
            for panel in range(panels - EXTRA, panels):
                k = 1 - x
                across(k, panel).wait_recv()
                if panel >= panels - TOP_EXTRA:
                    up(k, panel).start()
                else:

                    @pl.when(jnp.logical_not(is_near))
                    def _():
                        up(k, panel).start()

    def pass_high_end(distance):
        @pl.when((z + distance == last) & has_down)
        def _():
            for panel in range(panels - EXTRA, panels):
                k = last * PAIR + 1 - x
                across(k, panel).wait_recv()
                down(k, panel).start()

    def sends_done():
        @pl.loop(0, length)
        def sent(at):
            k = at * PAIR + x

            @pl.when(has_down & (at >= z))
            def _():
                wait_sent(1, k, 0, panels)

            short = is_near & (at >= last - NEAR) if far else False

            @pl.when(has_up & (at <= z) & jnp.logical_not(short))
            def _():
                wait_sent(0, k, 0, panels)

            @pl.when(has_up & (at <= z) & short)
            def _():
                wait_sent(0, k, 1, panels - 1)

            amount = end_panel(at) - first_panel(at)
            for size in sorted({panels, panels - 1, panels - EXTRA, panels - TOP_EXTRA}):

                @pl.when(amount == size)
                def _():
                    wait_sent(2, k, 0, size)

        @pl.when(has_up & is_near)
        def _():
            wait_sent(0, 1 - x, 0, TOP_EXTRA)

        @pl.when(has_up & jnp.logical_not(is_near))
        def _():
            wait_sent(0, 1 - x, 0, EXTRA)

        @pl.when(has_down)
        def _():
            wait_sent(1, last * PAIR + 1 - x, 0, EXTRA)

        if far:

            @pl.when(is_last)
            def _():
                for plane in range(NEAR):
                    far_down(plane).wait_send()

            @pl.when(is_near)
            def _():
                @pl.loop(1, cols // CORES)
                def peers(step):
                    who = (my_col + step * CORES) % cols
                    for plane in range(NEAR):
                        far_to(who, plane).wait_send()
                        far_move(who, plane, {"col": mate}, who, 1).wait_send()

                for plane in range(NEAR):
                    far_to(mate, plane).wait_send()

                far_result().wait_send()

    def split_in_two(value):
        high = value.astype(jnp.bfloat16)
        return high, (value - high.astype(jnp.float32)).astype(jnp.bfloat16)

    def right_of(at, panel):
        return gathered[pl.ds(at * PAIR, PAIR), panel].reshape(pair, block)

    def add_terms(distance):
        @pl.loop(0, 2)
        def each(way):
            at = z + (2 * way - 1) * distance

            @pl.when((at >= 0) & (at < length) & ((distance > 0) | ((distance == 0) & (way > 0))))
            def _():
                passed = ((at == 0) & has_up) | ((at == last) & has_down)

                first = first_panel(at)
                if far:
                    first = first + jnp.int32(is_near & (at >= last - NEAR) & (at < last))

                limit = panels - EXTRA * jnp.int32(passed)
                left_high = p_high[at]
                left_low = p_low[at]
                for begin in range(0, panels, GROUP):
                    for panel in range(begin, begin + GROUP):

                        @pl.when((panel >= first) & (panel < limit))
                        def _():
                            across(at * PAIR + 1 - x, panel).wait_recv()

                    right = jnp.concatenate(
                        [right_of(at, begin + panel) for panel in range(GROUP)], axis=1
                    )
                    high, low = split_in_two(right)
                    value = times(left_high, low) + times(left_low, high) + times(left_high, high)
                    here = slice(begin * block, (begin + GROUP) * block)
                    product[:, here] = product[:, here] + value

    def forward_far(plane):
        far_to(mate, plane).wait_recv()

        @pl.loop(1, cols // CORES)
        def peers(step):
            far_to((my_col + step * CORES) % cols, plane).start()

        far_to(mate, plane).start()

    def mate_far(plane):
        @pl.loop(1, cols // CORES)
        def peers(step):
            who = (my_col + step * CORES) % cols
            far_move(who, plane, {"col": mate}, who, 1).wait_recv()
            far_move(who, plane, {"col": mate}, who, 1).start()

    def give_far():
        @pl.loop(0, cols // CORES)
        def mates(step):
            who = (mate + step * CORES) % cols
            for plane in range(NEAR):
                far_move(who, plane, {"col": mate}, who).wait_recv()

        value = None
        for plane in range(NEAR):
            at = last - NEAR + plane
            across(at * PAIR + 1 - x, 0).wait_recv()
            left_high, left_low = split_in_two(p_far[:, plane * pair : (plane + 1) * pair])
            high, low = split_in_two(right_of(at, 0))
            one = times(left_high, low) + times(left_low, high) + times(left_high, high)
            value = one if value is None else value + one
        far_part[...] = value
        far_result().start()

    product[...] = jnp.zeros_like(product)
    inner = 0

    @pl.loop(0, length + 1)
    def steps(distance):
        for panel in range(panels):
            pass_below(distance + 1, panel)
            if far and panel >= panels - NEAR:

                @pl.when(is_near & (distance == 0))
                def _():
                    forward_far(panel - panels + NEAR)

                @pl.when(is_near & (distance == 1))
                def _():
                    mate_far(panel - panels + NEAR)

            ahead = panel + panels // 2
            pass_above(distance + ahead // panels, ahead % panels)

        pass_low_end(distance)
        pass_high_end(distance)
        if far:

            @pl.when(is_near & (distance == 1))
            def _():
                give_far()

        @pl.when(distance == length)
        def _():
            sends_done()

        add_terms(distance - 1 - inner)

    def squares_of(panel):
        part_of = product[:, panel * block : (panel + 1) * block]
        return jnp.sum((part_of * part_of).reshape(part_of.shape[0] // 8, 8, block), axis=0)

    mine = squares_of(1)
    for panel in range(2, panels):
        mine = mine + squares_of(panel)
    if far:

        @pl.when(is_last)
        def _():
            pltpu.make_async_copy(far_part, far_part, far_sem.at[1]).wait()
            product[:, 0:block] = product[:, 0:block] + far_part[...]

    mine = mine + squares_of(0)
    spot = me * cols + my_col
    parts[spot, 0:1] = jnp.sum(mine, axis=0, keepdims=True)

    def part(slot, device):
        return pltpu.make_async_remote_copy(
            src_ref=parts.at[slot, pl.ds(0, 1)],
            dst_ref=parts.at[slot, pl.ds(0, 1)],
            send_sem=part_sem.at[0],
            recv_sem=part_sem.at[1],
            device_id={"blk": device // cols, "col": device % cols},
            device_id_type=MESH,
        )

    @pl.loop(0, total)
    def send_parts(device):
        @pl.when(device != spot)
        def _():
            part(spot, device).start()

    others = parts.at[pl.ds(0, total - 1), pl.ds(0, 1)]
    pltpu.make_async_copy(others, others, part_sem.at[0]).wait()
    pltpu.make_async_copy(others, others, part_sem.at[1]).wait()
    norm[...] = jnp.sum(parts[:, 0, :], axis=0, keepdims=True)


def finish(product_in, norm_in, product_out, norm_out, value, sem):
    store = pltpu.make_async_copy(product_in, product_out, sem.at[0])
    store.start()
    value[0] = jnp.sum(norm_in[...])
    send = pltpu.make_async_copy(value, norm_out, sem.at[1])
    send.start()
    store.wait()
    send.wait()


def solution(mesh):
    count = mesh.shape["blk"]
    cols = mesh.shape["col"]
    length = count // PAIR

    def per_device(
        density,
        occupied_p,
        hamil_dens,
        occupied_hp,
        window_sizes,
        row_window_sizes,
        slab_index,
        group_sizes,
    ):
        rows, inner = density.shape
        block, width = hamil_dens.shape
        hbm = pl.BlockSpec(memory_space=pltpu.HBM)
        vmem = pl.BlockSpec(memory_space=pltpu.VMEM)
        smem = pl.BlockSpec(memory_space=pltpu.SMEM)
        product, norm = pl.pallas_call(
            functools.partial(kernel, length, cols),
            out_shape=(
                pltpu.VMEM((rows, width), jnp.float32),
                pltpu.VMEM((1, 128), jnp.float32),
            ),
            in_specs=[hbm] * 8,
            out_specs=(vmem, vmem),
            scratch_shapes=[
                pltpu.VMEM((block, width), jnp.float32),
                pltpu.SMEM(occupied_p.shape, jnp.int32),
                pltpu.SMEM(occupied_hp.shape, jnp.int32),
                pltpu.SMEM(window_sizes.shape, jnp.int32),
                pltpu.SMEM(row_window_sizes.shape, jnp.int32),
                pltpu.SMEM(slab_index.shape, jnp.int32),
                pltpu.SMEM(group_sizes.shape, jnp.int32),
                pltpu.VMEM((count, width // block, block, block), jnp.float32),
                pltpu.VMEM((rows, inner), jnp.float32),
                pltpu.VMEM((length, rows, PAIR * block), jnp.bfloat16),
                pltpu.VMEM((length, rows, PAIR * block), jnp.bfloat16),
                pltpu.VMEM((rows, NEAR * PAIR * block), jnp.float32),
                pltpu.VMEM((rows, block), jnp.float32),
                pltpu.VMEM((count * cols, 8, 128), jnp.float32),
                pltpu.SemaphoreType.DMA((3, count)),
                pltpu.SemaphoreType.DMA((count, width // block)),
                pltpu.SemaphoreType.DMA((7 + width // block,)),
                pltpu.SemaphoreType.DMA((2,)),
                pltpu.SemaphoreType.DMA((2, cols, NEAR)),
                pltpu.SemaphoreType.DMA((cols, NEAR)),
                pltpu.SemaphoreType.DMA((2,)),
            ],
            compiler_params=pltpu.CompilerParams(
                collective_id=0, has_side_effects=True, vmem_limit_bytes=56 << 20
            ),
        )(
            *(
                pltpu.with_memory_space_constraint(value, pltpu.HBM)
                for value in (
                    density,
                    hamil_dens,
                    occupied_p,
                    occupied_hp,
                    window_sizes,
                    row_window_sizes,
                    slab_index,
                    group_sizes,
                )
            )
        )
        product, norm = pl.pallas_call(
            finish,
            out_shape=(
                jax.ShapeDtypeStruct((rows, width), jnp.float32),
                jax.ShapeDtypeStruct((1,), jnp.float32),
            ),
            in_specs=[vmem, vmem],
            out_specs=(hbm, hbm),
            scratch_shapes=[pltpu.SMEM((1,), jnp.float32), pltpu.SemaphoreType.DMA((2,))],
            compiler_params=pltpu.CompilerParams(vmem_limit_bytes=1 << 20),
        )(pltpu.with_memory_space_constraint(product, pltpu.VMEM), pltpu.with_memory_space_constraint(norm, pltpu.VMEM))
        return product, norm.reshape(())

    return jax.shard_map(
        per_device,
        mesh=mesh,
        in_specs=(
            P("blk", None),
            P("blk", None),
            P("blk", "col"),
            P("blk", "col"),
            P(),
            P(),
            P("col"),
            P(),
        ),
        out_specs=(P("blk", "col"), P()),
        check_vma=False,
    )
```
